256 devices in a mesh: group: 8 (over z_lo, y), dev: 32 (over z_hi, x, core).
Axes of the slice: x: 4, y: 4, z: 8 (z_hi: 4, z_lo: 2; z = z_hi * 2 + z_lo), core: 2. Of those that a mesh axis runs over, the one named last changes fastest.
Arguments:
- tiles: bfloat16 [256, 256, 1280], P(('group', 'dev')), may hold values from -6 to 6
- w_qkv: bfloat16 [1280, 3840], P('dev'), may hold values from -0.15625 to 0.15625
- w_out: bfloat16 [1280, 1280], replicated, may hold values from -0.15625 to 0.15625
- w_kv: bfloat16 [1280, 1024], replicated, may hold values from -0.15625 to 0.15625
- ln_gain: float32 [1280], replicated, may hold values from 0.25 to 1.75
- ln_bias: float32 [1280], replicated, may hold values from -2 to 2
- k_gain: float32 [128], replicated, may hold values from 0.5 to 2
- cross_queries: bfloat16 [16384, 4096], P(('group', 'dev')), may hold values from -110 to 110
- self_queries: bfloat16 [16384, 4096], P(('group', 'dev')), may hold values from -110 to 110
- text_kv: bfloat16 [16384, 1024], P(('group', 'dev')), may hold values from -6 to 6
- tiles_per_image: int32 [8, 16], replicated, may hold values from 1 to 4, 32 in all within a row
- request_table: int32 [8, 2], replicated, may hold values from 0 to 127
- span_offsets: int32 [8], replicated, may hold values from 0 to 2047
Outputs:
- cross_context: bfloat16 [16384, 4096], P(('group', 'dev'))
- self_context: bfloat16 [16384, 4096], P(('group', 'dev'))
The draws below stay inside these ranges and needn't reach their ends.
Inputs may be any that keep to these rules, and one draw needn't show every extreme that they name: `tiles_per_image`: each row sums to 32; some image has exactly 4 tiles.
All inputs are finite; a program needn't handle non-finite values.
Results may differ from the reference program's by a relative error of at most 0.03.
Values may be sent and summed in bfloat16 or wider, within the bound.
No kernel may reach another device: no remote copies, remote signals or barrier semaphores. Data moves between devices by JAX's collectives and lax.ppermute only.
A program may use at most 64 MiB of HBM per device.

```python
import math
import jax
import jax.numpy as jnp
import numpy as np
from jax import lax

DV = 1280
VH = 16
VHD = 80
HQ = 32
KVH = 4
HD = 128
TILE_ROWS = 256
SLOTS = 2
MAXT = 4
TILES_G = 32
IMG_G = 16
IMAGES = 128
TILES = 256
SPAN = 2048
TOKENS = 16384
N_GROUP = 8


def draw_cross_queries(key, part):
    key = jax.random.fold_in(key, 7)
    first_key = jax.random.fold_in(key, 0)
    base = jnp.clip(jax.random.normal(first_key, (TOKENS, HQ * HD), jnp.float32), -6.0, 6.0)
    return base.astype(jnp.bfloat16)


def draw_self_queries(key, part):
    key = jax.random.fold_in(key, 13)
    first_key = jax.random.fold_in(key, 0)
    base = jnp.clip(jax.random.normal(first_key, (TOKENS, HQ * HD), jnp.float32), -6.0, 6.0)
    return base.astype(jnp.bfloat16)


def place_ends(drawn, stream_key, smallest, top_value):
    dims = drawn.shape
    index_at = [jax.random.randint(jax.random.fold_in(stream_key, axis), (), 0, dims[axis]) for axis in range(len(dims))]
    drawn = drawn.at[tuple(index_at)].set(smallest)
    longest = dims.index(max(dims))
    index_at[longest] = (index_at[longest] + 1) % dims[longest]
    return drawn.at[tuple(index_at)].set(top_value)


def steps_of(stream_key, dims, cuts, low, largest):
    level = 1.0
    for dim, parts in cuts:
        draws = jax.random.uniform(jax.random.fold_in(jax.random.fold_in(stream_key, 6), dim), (parts,), jnp.float32, low / len(cuts), largest / len(cuts))
        level = level * jnp.repeat(jnp.exp(draws), dims[dim] // parts).reshape((-1,) + (1,) * (len(dims) - 1 - dim))
    return level


def rank_table(count, slope):
    loads = [(1 << 20) // math.isqrt(rank ** slope) + 1 for rank in range(1, count + 1)]
    deviation = 1 + sum(loads) // (1 << 30)
    return np.cumsum(np.array([max(1, weight // deviation) for weight in loads]))


def ranked_ids(own_key, extent, count, skew):
    table = rank_table(count, skew)
    lot = jax.random.randint(jax.random.fold_in(own_key, 1), extent, 0, int(table[count - 1]))
    rank = jnp.searchsorted(jnp.asarray(table, jnp.int32), lot, side="right")
    return jax.random.permutation(jax.random.fold_in(own_key, 2), count)[rank].astype(jnp.int32)


def split_up(count, total, reach, slope):
    portions = [(1 << 20) // math.isqrt(standing ** slope) + 1 for standing in range(2, count + 1)]
    surplus, holding = total - reach - (count - 1), [1] * (count - 1)
    while surplus > 0:
        candidates = [i for i in range(count - 1) if holding[i] < reach]
        pool, budget = sum([portions[i] for i in candidates]), surplus
        for i in candidates:
            addition = min(reach - holding[i], max(1, budget * portions[i] // pool), surplus)
            holding[i] = holding[i] + addition
            surplus = surplus - addition
    return np.array([reach] + holding)


def ragged_sizes(key, count, total, reach, lean):
    if count == 2:
        one = jax.random.randint(key, (), max(1, total - reach), min(reach, total - 1) + 1)
        return jnp.stack([one, total - one])
    sizes = jnp.asarray(split_up(count, total, reach, lean), jnp.int32)
    twos = (count - 1) // 2
    donor, taker = sizes[1:1 + 2 * twos:2], sizes[2:2 + 2 * twos:2]
    margin = jnp.minimum(donor - 1, reach - taker)
    moved = jax.random.randint(jax.random.fold_in(key, 1), (twos,), 0, 1 << 20) % (margin + 1)
    sizes = sizes.at[1:1 + 2 * twos:2].set(donor - moved).at[2:2 + 2 * twos:2].set(taker + moved)
    return sizes[jax.random.permutation(jax.random.fold_in(key, 2), count)]


def scatter_about(own_key, dims, scale, limit, cuts=(), held_as=jnp.bfloat16):
    loudness = steps_of(own_key, dims, cuts, -0.22, 0.18) if cuts else 1.0
    drawn = jax.random.normal(own_key, dims, jnp.float32) * scale * loudness
    return jnp.minimum(jnp.maximum(drawn, -limit), limit).astype(held_as)


def setup_inputs(seed: int = 0) -> dict:
    key_list = jax.random.split(jax.random.key(seed), 14)
    return {
        "tiles": scatter_about(key_list[0], (TILES, TILE_ROWS, DV), 1.0, 6.0, ((0, 256),)),
        "w_qkv": scatter_about(key_list[1], (DV, 3 * DV), DV ** -0.5, 0.15625, ((0, 32),)),
        "w_out": scatter_about(key_list[2], (DV, DV), DV ** -0.5, 0.15625),
        "w_kv": scatter_about(key_list[3], (DV, 2 * KVH * HD), DV ** -0.5, 0.15625),
        "ln_gain": jnp.clip(1.0 + 0.15 * jax.random.normal(key_list[4], (DV,), jnp.float32), 0.25, 1.75),
        "ln_bias": scatter_about(key_list[5], (DV,), 0.4, 2.0, (), jnp.float32),
        "k_gain": jnp.clip(jnp.exp(jax.random.uniform(key_list[6], (HD,), jnp.float32, math.log(0.5), math.log(2.0))), 0.5, 2.0),
        "cross_queries": draw_cross_queries(jax.random.fold_in(key_list[13], 71), 0),
        "self_queries": draw_self_queries(jax.random.fold_in(key_list[13], 71), 0),
        "text_kv": scatter_about(key_list[9], (TOKENS, 2 * KVH * HD), 1.0, 6.0, ((0, 256),)),
        "tiles_per_image": jax.vmap(lambda own: ragged_sizes(own, IMG_G, TILES_G, MAXT, 1))(jax.random.split(key_list[10], N_GROUP)).reshape((N_GROUP, IMG_G)).astype(jnp.int32),
        "request_table": place_ends(ranked_ids(key_list[11], (N_GROUP, SLOTS), IMAGES, 2), jax.random.fold_in(key_list[11], 3), 0, IMAGES - 1).astype(jnp.int32),
        "span_offsets": place_ends(jax.random.randint(key_list[12], (N_GROUP,), 0, SPAN), jax.random.fold_in(key_list[12], 1), 0, SPAN - 1).astype(jnp.int32),
    }


def layer_norm(values, gain, bias):
    widened = values.astype(jnp.float32)
    center = lax.optimization_barrier(jnp.mean(widened, axis=-1, keepdims=True))
    spread = lax.optimization_barrier(jnp.mean(jnp.square(widened - center), axis=-1, keepdims=True))
    return ((widened - center) * lax.rsqrt(spread + 1e-05) * gain + bias).astype(jnp.bfloat16)

def tile_attention(qkv_out):
    row_count = qkv_out.shape[0]
    sections = qkv_out.reshape(row_count, 3, VH, VHD).astype(jnp.float32)
    scores = jnp.einsum('qhd,khd->hqk', sections[:, 0], sections[:, 1]) / math.sqrt(VHD)
    highest = lax.optimization_barrier(jnp.max(scores, axis=-1, keepdims=True))
    exponent = jnp.exp(scores - highest)
    weights = (exponent / lax.optimization_barrier(jnp.sum(exponent, axis=-1, keepdims=True))).astype(jnp.bfloat16)
    context = jnp.einsum('hqk,khd->qhd', weights.astype(jnp.float32), sections[:, 2])
    return context.reshape(row_count, VH * VHD).astype(jnp.bfloat16)

def finish_tile(tile_rows, context, w_out, w_kv, k_gain):
    residual_sum = (tile_rows.astype(jnp.float32) + jnp.dot(context, w_out, preferred_element_type=jnp.float32)).astype(jnp.bfloat16)
    projected = jnp.dot(residual_sum, w_kv, preferred_element_type=jnp.float32)
    row_count = projected.shape[0]
    key_part = projected[:, :KVH * HD].reshape(row_count, KVH, HD)
    key_part = key_part * lax.rsqrt(lax.optimization_barrier(jnp.mean(jnp.square(key_part), axis=-1, keepdims=True)) + 1e-06) * k_gain
    return jnp.concatenate([key_part.reshape(row_count, KVH * HD), projected[:, KVH * HD:]], axis=1).astype(jnp.bfloat16)

def attend(queries, keyvals, key_mask):
    row_count = queries.shape[0]
    key_count = keyvals.shape[0]
    group_size = HQ // KVH
    query_part = queries.reshape(row_count, KVH, group_size, HD).transpose(1, 0, 2, 3)
    key_part = keyvals[:, :KVH * HD].reshape(key_count, KVH, HD).transpose(1, 0, 2)
    value_part = keyvals[:, KVH * HD:].reshape(key_count, KVH, HD).transpose(1, 0, 2)

    def one_head(operand):
        query_head, key_head, value_head = operand
        scores = jnp.einsum('rgd,kd->grk', query_head.astype(jnp.float32), key_head.astype(jnp.float32)) / math.sqrt(HD)
        highest = lax.optimization_barrier(jnp.max(jnp.where(key_mask, scores, -jnp.inf), axis=-1, keepdims=True))
        exponent = jnp.where(key_mask, jnp.exp(scores - highest), 0.0)
        weights = (exponent / lax.optimization_barrier(jnp.sum(exponent, axis=-1, keepdims=True))).astype(jnp.bfloat16)
        return jnp.einsum('grk,kd->rgd', weights.astype(jnp.float32), value_head.astype(jnp.float32))
    outputs = lax.map(one_head, (query_part, key_part, value_part))
    return outputs.transpose(1, 0, 2, 3).reshape(row_count, HQ * HD).astype(jnp.bfloat16)

def reference(tiles, w_qkv, w_out, w_kv, ln_gain, ln_bias, k_gain, cross_queries, self_queries, text_kv, tiles_per_image, request_table, span_offsets):

    def encode(tile_rows):
        normed = layer_norm(tile_rows, ln_gain, ln_bias)
        qkv_out = jnp.dot(normed, w_qkv, preferred_element_type=jnp.float32).astype(jnp.bfloat16)
        return finish_tile(tile_rows, tile_attention(qkv_out), w_out, w_kv, k_gain)
    image_kv = lax.map(encode, tiles)
    flat_tiles = tiles_per_image.reshape(-1)
    starts = (jnp.cumsum(tiles_per_image, axis=1) - tiles_per_image).reshape(-1).astype(jnp.int32)
    tile_step = jnp.arange(MAXT, dtype=jnp.int32)
    slot_index = jnp.arange(SLOTS * MAXT, dtype=jnp.int32) // MAXT
    span_rows = jnp.arange(SPAN, dtype=jnp.int32)

    def one_group(operand):
        image_ids, offset, queries, own_queries, own_kv = operand
        counts = flat_tiles[image_ids]
        first_tile = starts[image_ids]
        owner_group = image_ids // IMG_G
        is_valid = (tile_step[None, :] < counts[:, None]).reshape(-1)
        global_tile = (owner_group[:, None] * TILES_G + first_tile[:, None] + tile_step[None, :]).reshape(-1)
        global_tile = jnp.minimum(global_tile, TILES - 1).astype(jnp.int32)
        picked = jnp.where(is_valid[:, None, None], image_kv[global_tile], jnp.zeros((), image_kv.dtype))
        keyvals = picked.reshape(SLOTS * MAXT * TILE_ROWS, 2 * KVH * HD)
        position = offset + span_rows
        visible = (position[:, None] >= slot_index[None, :] * (SPAN // SLOTS)) & is_valid[None, :]
        key_mask = jnp.repeat(visible, TILE_ROWS, axis=1)
        cross_out = attend(queries, keyvals, key_mask)
        causal = span_rows[:, None] >= span_rows[None, :]
        self_out = attend(own_queries, own_kv, causal)
        return (cross_out, self_out)
    cross_out, self_out = lax.map(one_group, (request_table, span_offsets, cross_queries.reshape(N_GROUP, SPAN, HQ * HD), self_queries.reshape(N_GROUP, SPAN, HQ * HD), text_kv.reshape(N_GROUP, SPAN, 2 * KVH * HD)))
    return (cross_out.reshape(TOKENS, HQ * HD), self_out.reshape(TOKENS, HQ * HD))
```

```python
import math

import jax
import jax.numpy as jnp
from jax import lax
from jax.experimental import pallas as pl
from jax.experimental.pallas import tpu as pltpu
from jax.sharding import PartitionSpec as P

RING = 4
VHD = 80
HD = 128
KVH = 4
GQ = 8
SLOTS = 2
IMG_G = 16
TILE_ROWS = 256
DV = 1280
PART = 480
HALF = 160
SLOT_SPAN = 1024
LOG2E = math.log2(math.e)
LOW = -1e30
BF = jnp.bfloat16
F32 = jnp.float32
VM = pl.BlockSpec(memory_space=pltpu.VMEM)
SM = pl.BlockSpec(memory_space=pltpu.SMEM)


def shape(rows, cols):
    return jax.ShapeDtypeStruct((rows, cols), BF)


def call(body, outs, scalars, arrays, scratch=(), limit=40, flops=0):
    return pl.pallas_call(
        body,
        out_shape=outs,
        in_specs=[SM] * len(scalars) + [VM] * len(arrays),
        out_specs=[VM] * len(outs),
        scratch_shapes=list(scratch),
        compiler_params=pltpu.CompilerParams(vmem_limit_bytes=limit << 20),
        cost_estimate=pl.CostEstimate(flops=flops, bytes_accessed=1 << 20, transcendentals=0),
    )(*scalars, *arrays)


def x_shift(value, k):
    return lax.ppermute(value, "dev", [(i, (i // 8) * 8 + (i + 2 * k) % 8) for i in range(32)])


def z_shift(value, k):
    return lax.ppermute(value, "dev", [(i, (i + 8 * k) % 32) for i in range(32)])


def core_swap(value):
    return lax.ppermute(value, "dev", [(i, i ^ 1) for i in range(32)])


def aligned(value, unit):
    return pl.multiple_of(value * unit, unit)


def split_tile_body(pos, tile, *outs):
    for k in range(RING):
        outs[k][...] = tile[pl.ds(aligned((pos[1] + k) % RING, 64), 64), :]


def pack_body(pos, *refs):
    ins, outs = refs[:RING], refs[RING:]
    for k in range(RING):
        for j in range(RING):
            outs[k][16 * j : 16 * j + 16, :] = ins[j][pl.ds(aligned((pos[0] + k) % RING, 16), 16), :]


def first_of(tpi, image):
    row, col = image // IMG_G, image % IMG_G
    total = jnp.int32(0)
    for j in range(IMG_G):
        total = total + jnp.where(j < col, tpi[row * IMG_G + j], 0)
    return total


def select_body(pos, tpi, table, *refs):
    ins, out, held = refs[:RING], refs[RING], refs[RING + 1]
    for k in range(RING):
        held[64 * k : 64 * k + 64, :] = ins[k][...]
    for item in range(8 * SLOTS):
        first = first_of(tpi, table[item])
        for u in range(2):
            step = ((pos[2] + first) & 1) + 2 * u
            chip = jnp.minimum(first + step, 31) // 2
            zk = (pos[0] - chip // RING + RING) % RING
            xk = (pos[1] - chip % RING + RING) % RING
            row = (item * 2 + u) * 16
            out[row : row + 16, :] = held[pl.ds(aligned(zk * RING + xk, 16), 16), :]


def pick_body(pos, table, *refs):
    for k in range(RING):
        refs[RING + k][...] = refs[k][...]


def pick(pos, table, received):
    def at(k):
        def index(i, pos, table):
            entry = (pos[0] + k) % RING
            return ((table[pos[3] * SLOTS + entry // 2] // IMG_G) * RING + entry, 0)

        return pl.BlockSpec((16, DV), index)

    return pl.pallas_call(
        pick_body,
        out_shape=[shape(16, DV)] * RING,
        grid_spec=pltpu.PrefetchScalarGridSpec(
            num_scalar_prefetch=2,
            grid=(1,),
            in_specs=[at(k) for k in range(RING)],
            out_specs=[pl.BlockSpec((16, DV), lambda i, pos, table: (0, 0))] * RING,
        ),
    )(pos, table, *([received] * RING))


def split_w_body(pos, w, mine, theirs):
    first = pos[2] == 0
    for p in range(RING):
        for j in range(3):
            at = j * DV + p * 2 * HALF
            lo, hi = w[:, at : at + HALF], w[:, at + HALF : at + 2 * HALF]
            mine[p, :, j * HALF : (j + 1) * HALF] = jnp.where(first, lo, hi)
            theirs[p, :, j * HALF : (j + 1) * HALF] = jnp.where(first, hi, lo)


def split_cols_body(pos, kv, cq, *outs):
    for k in range(RING):
        head = (pos[1] + k) % RING
        outs[k][:, :HD] = kv[:, pl.ds(aligned(head, HD), HD)]
        outs[k][:, HD:] = kv[:, pl.ds(aligned(head + KVH, HD), HD)]
        outs[RING + k][...] = cq[:, pl.ds(aligned(head, GQ * HD), GQ * HD)]


def assemble_rows(pos, blocks, tile):
    for k in range(RING):
        tile[pl.ds(aligned((pos[1] - k + RING) % RING, 64), 64), :] = blocks[k][...]


def encode_body(pos, gain, bias, *refs):
    blocks, weights = refs[:RING], refs[RING : 3 * RING]
    out, tile, held = refs[3 * RING], refs[3 * RING + 1], refs[3 * RING + 2 :]
    assemble_rows(pos, blocks, tile)
    for half in range(2):
        for zk in range(RING):
            for xk in range(RING):
                row = ((pos[0] - zk + RING) % RING) * RING + (pos[1] - xk + RING) % RING
                held[half][pl.ds(aligned(row, 80), 80), :] = weights[half * RING + zk][80 * xk : 80 * xk + 80, :]
    value = tile[...].astype(F32)
    center = jnp.mean(value, axis=-1, keepdims=True)
    value = value - center
    spread = jnp.mean(jnp.square(value), axis=-1, keepdims=True)
    normed = (value * lax.rsqrt(spread + 1e-05) * gain[...] + bias[...]).astype(BF)
    lane = lax.broadcasted_iota(jnp.int32, (TILE_ROWS, HALF), 1)
    scale = LOG2E / math.sqrt(VHD)
    for half in range(2):
        qkv = jnp.dot(normed, held[half][...], preferred_element_type=F32).astype(BF)
        query, key, value = qkv[:, :HALF], qkv[:, HALF : 2 * HALF], qkv[:, 2 * HALF :]
        context = jnp.zeros((TILE_ROWS, HALF), F32)
        for h in range(2):
            mine = (lane < VHD) == (h == 0)
            zero = jnp.zeros((), BF)
            scores = lax.dot_general(
                jnp.where(mine, query, zero), key, (((1,), (1,)), ((), ())), preferred_element_type=F32
            )
            highest = jnp.max(scores, axis=-1, keepdims=True)
            exponent = jnp.exp2((scores - highest) * scale)
            total = jnp.sum(exponent, axis=-1, keepdims=True)
            weight = (exponent / total).astype(BF)
            context = context + jnp.dot(weight, jnp.where(mine, value, zero), preferred_element_type=F32)
        out[:, half * HALF : (half + 1) * HALF] = context.astype(BF)


def project_body(pos, k_gain, w_out, w_kv, *refs):
    blocks, contexts = refs[:RING], refs[RING : 2 * RING]
    out, tile, held = refs[2 * RING :]
    assemble_rows(pos, blocks, tile)
    total = tile[...].astype(F32)
    for k in range(RING):
        part = (pos[1] - k + RING) % RING
        held[:HALF, :] = w_out[pl.ds(aligned(part * 2 + pos[2], HALF), HALF), :]
        held[HALF:, :] = w_out[pl.ds(aligned(part * 2 + 1 - pos[2], HALF), HALF), :]
        total = total + jnp.dot(contexts[k][...], held[...], preferred_element_type=F32)
    residual = total.astype(BF)
    key = jnp.dot(residual, w_kv[:, pl.ds(aligned(pos[1], HD), HD)], preferred_element_type=F32)
    value = jnp.dot(residual, w_kv[:, pl.ds(aligned(pos[1] + KVH, HD), HD)], preferred_element_type=F32)
    key = key * lax.rsqrt(jnp.mean(jnp.square(key), axis=-1, keepdims=True) + 1e-06) * k_gain[...]
    out[:, :HD] = key.astype(BF)
    out[:, HD:] = value.astype(BF)


BLOCK = 256


def softmax_rows(query, keys, values, seen):
    scores = lax.dot_general(query, keys, (((1,), (1,)), ((), ())), preferred_element_type=F32)
    scores = seen(scores)
    highest = jnp.max(scores, axis=-1, keepdims=True)
    exponent = jnp.exp2((scores - highest) * (LOG2E / math.sqrt(HD)))
    total = jnp.sum(exponent, axis=-1, keepdims=True)
    result = jnp.dot(exponent.astype(BF), values, preferred_element_type=F32)
    return (result / total).astype(BF)


def cross_body(pos, tpi, table, offsets, *refs):
    queries, pieces = refs[:RING], refs[RING : 3 * RING]
    outs = refs[3 * RING : 4 * RING]
    held_q, held_o, held_k, held_v = refs[4 * RING :]
    for k in range(RING):
        for h in range(GQ):
            held_q[(k * GQ + h) * 64 : (k * GQ + h + 1) * 64, :] = queries[k][:, h * HD : (h + 1) * HD]
    for n in range(2 * RING):
        held_k[n * TILE_ROWS : (n + 1) * TILE_ROWS, :] = pieces[n][:, :HD]
        held_v[n * TILE_ROWS : (n + 1) * TILE_ROWS, :] = pieces[n][:, HD:]
    group = pos[3]
    slot_of, low_of = [], []
    images = [table[group * SLOTS + s] for s in range(SLOTS)]
    firsts = [first_of(tpi, image) for image in images]
    counts = [tpi[image] for image in images]
    for n in range(2 * RING):
        entry = (pos[0] - n % RING + RING) % RING
        slot, u = entry // 2, entry % 2
        core = pos[2] if n < RING else 1 - pos[2]
        first = jnp.where(slot == 0, firsts[0], firsts[1])
        count = jnp.where(slot == 0, counts[0], counts[1])
        step = ((core + first) & 1) + 2 * u
        slot_of.append(slot)
        low_of.append(jnp.where(step < count, 0.0, LOW).astype(F32))

    def block(i, carry):
        at = pl.ds(pl.multiple_of(i * BLOCK, BLOCK), BLOCK)
        source = (pos[1] - i // (GQ * 64 // BLOCK) + RING) % RING
        start = offsets[group] + pos[0] * 512 + source * 128 + pos[2] * 64
        row = lax.broadcasted_iota(jnp.int32, (BLOCK, 1), 0)
        position = start + row % 64

        def seen(scores):
            parts = []
            for n in range(2 * RING):
                low = jnp.where(position >= slot_of[n] * SLOT_SPAN, low_of[n], LOW)
                parts.append(scores[:, n * TILE_ROWS : (n + 1) * TILE_ROWS] + low)
            return jnp.concatenate(parts, axis=1)

        held_o[at, :] = softmax_rows(held_q[at, :], held_k[...], held_v[...], seen)
        return carry

    lax.fori_loop(0, RING * GQ * 64 // BLOCK, block, 0)
    for k in range(RING):
        for h in range(GQ):
            outs[k][:, h * HD : (h + 1) * HD] = held_o[(k * GQ + h) * 64 : (k * GQ + h + 1) * 64, :]


def self_body(pos, queries, kv, out, held_q, held_o):
    span = kv.shape[0]
    rows = queries.shape[0]
    for h in range(KVH * GQ):
        held_q[h * rows : (h + 1) * rows, :] = queries[:, h * HD : (h + 1) * HD]
    start = ((pos[0] * RING + pos[1]) * 2 + pos[2]) * rows

    def block(i, carry):
        at = pl.ds(pl.multiple_of(i * BLOCK, BLOCK), BLOCK)
        head = i // (GQ * rows // BLOCK)
        keys = kv[:, pl.ds(aligned(head, HD), HD)]
        values = kv[:, pl.ds(aligned(head + KVH, HD), HD)]
        row = start + lax.broadcasted_iota(jnp.int32, (BLOCK, 1), 0) % rows
        col = lax.broadcasted_iota(jnp.int32, (1, span), 1)
        held_o[at, :] = softmax_rows(
            held_q[at, :], keys, values, lambda scores: jnp.where(col <= row, scores, LOW)
        )
        return carry

    lax.fori_loop(0, KVH * GQ * rows // BLOCK, block, 0)
    for h in range(KVH * GQ):
        out[:, h * HD : (h + 1) * HD] = held_o[h * rows : (h + 1) * rows, :]


def place_body(pos, *refs):
    ins, out = refs[:RING], refs[RING]
    for k in range(RING):
        out[:, pl.ds(aligned((pos[1] + k) % RING, GQ * HD), GQ * HD)] = ins[k][...]


def per_device(
    tiles,
    w_qkv,
    w_out,
    w_kv,
    ln_gain,
    ln_bias,
    k_gain,
    cross_queries,
    self_queries,
    text_kv,
    tiles_per_image,
    request_table,
    span_offsets,
):
    dev = lax.axis_index("dev")
    pos = jnp.stack([dev // 8, (dev // 2) % 4, dev % 2, lax.axis_index("group")]).astype(jnp.int32)
    tpi = tiles_per_image.reshape(-1)
    table = request_table.reshape(-1)
    span_kv = lax.all_gather(text_kv, "dev", axis=0, tiled=True)

    blocks = call(split_tile_body, [shape(64, DV)] * RING, (pos,), (tiles.reshape(TILE_ROWS, DV),))
    spread = [blocks[0]] + [x_shift(blocks[k], k) for k in (1, 2, 3)]

    mine, theirs = pl.pallas_call(
        split_w_body,
        out_shape=[jax.ShapeDtypeStruct((RING, 40, PART), BF)] * 2,
        in_specs=[SM, VM],
        out_specs=[VM] * 2,
    )(pos, w_qkv)
    got = core_swap(theirs)
    even = pos[2] == 0
    pair = jnp.concatenate([jnp.where(even, mine, got), jnp.where(even, got, mine)], axis=1)
    parts = [lax.dynamic_index_in_dim(pair, (pos[1] + k) % RING, 0, keepdims=False) for k in range(RING)]
    parts = jnp.concatenate([parts[0]] + [x_shift(parts[k], k) for k in (1, 2, 3)], axis=0)

    cols = call(
        split_cols_body,
        [shape(64, 2 * HD)] * RING + [shape(64, GQ * HD)] * RING,
        (pos,),
        (text_kv, cross_queries),
    )
    cq = [cols[RING]] + [x_shift(cols[RING + k], k) for k in (1, 2, 3)]

    packed = call(pack_body, [shape(64, DV)] * RING, (pos,), tuple(spread))
    packed = [packed[0]] + [z_shift(packed[k], k) for k in (1, 2, 3)]
    weights = [parts] + [z_shift(parts, k) for k in (1, 2, 3)]

    chosen = call(
        select_body,
        [shape(8 * 64, DV)],
        (pos, tpi, table),
        tuple(packed),
        [pltpu.VMEM((TILE_ROWS, DV), BF)],
    )[0]
    received = lax.all_to_all(chosen.reshape(8, 64, DV), "group", 0, 0, tiled=True).reshape(8 * 64, DV)
    picked = pick(pos, table, received)
    rows = jnp.concatenate([picked[0]] + [z_shift(picked[k], k) for k in (1, 2, 3)], axis=0)
    blocks = [rows] + [x_shift(rows, k) for k in (1, 2, 3)]

    weights = weights + [core_swap(value) for value in weights]
    context = call(
        encode_body,
        [shape(TILE_ROWS, 2 * HALF)],
        (pos,),
        (ln_gain.reshape(1, DV), ln_bias.reshape(1, DV), *blocks, *weights),
        [pltpu.VMEM((TILE_ROWS, DV), BF), pltpu.VMEM((DV, PART), BF), pltpu.VMEM((DV, PART), BF)],
        flops=1 << 30,
    )[0]
    contexts = [context] + [x_shift(context, k) for k in (1, 2, 3)]
    piece = call(
        project_body,
        [shape(TILE_ROWS, 2 * HD)],
        (pos,),
        (k_gain.reshape(1, HD), w_out, w_kv, *blocks, *contexts),
        [pltpu.VMEM((TILE_ROWS, DV), BF), pltpu.VMEM((2 * HALF, DV), BF)],
        flops=1 << 30,
    )[0]
    pieces = [piece] + [z_shift(piece, k) for k in (1, 2, 3)]
    pieces = pieces + [core_swap(value) for value in pieces]
    stack = RING * GQ * 64
    tokens = cross_queries.shape[0]
    back = call(
        cross_body,
        [shape(64, GQ * HD)] * RING,
        (pos, tpi, table, span_offsets),
        (*cq, *pieces),
        [pltpu.VMEM((stack, HD), BF)] * 4,
        flops=1 << 32,
    )
    back = [back[0]] + [x_shift(back[k], RING - k) for k in (1, 2, 3)]
    cross_out = call(place_body, [shape(tokens, RING * GQ * HD)], (pos,), tuple(back))[0]
    self_out = call(
        self_body,
        [shape(tokens, KVH * GQ * HD)],
        (pos,),
        (self_queries, span_kv),
        [pltpu.VMEM((stack, HD), BF)] * 2,
        flops=1 << 32,
    )[0]
    return (cross_out, self_out)


def solution(mesh):
    in_specs = (
        P(("group", "dev"), None, None),
        P("dev", None),
        P(),
        P(),
        P(),
        P(),
        P(),
        P(("group", "dev"), None),
        P(("group", "dev"), None),
        P(("group", "dev"), None),
        P(),
        P(),
        P(),
    )
    out_specs = (P(("group", "dev"), None), P(("group", "dev"), None))
    return jax.shard_map(
        per_device, mesh=mesh, in_specs=in_specs, out_specs=out_specs, check_vma=False
    )
```

```python
import math

import jax
import jax.numpy as jnp
from jax import lax
from jax.experimental import pallas as pl
from jax.experimental.pallas import tpu as pltpu
from jax.sharding import PartitionSpec as P

RING = 4
VHD = 80
HD = 128
KVH = 4
GQ = 8
SLOTS = 2
IMG_G = 16
TILE_ROWS = 256
DV = 1280
PART = 480
WIDE = 512
HALF = 160
SLOT_SPAN = 1024
LOG2E = math.log2(math.e)
LOW = -1e30
BF = jnp.bfloat16
F32 = jnp.float32
VM = pl.BlockSpec(memory_space=pltpu.VMEM)
SM = pl.BlockSpec(memory_space=pltpu.SMEM)


def shape(rows, cols):
    return jax.ShapeDtypeStruct((rows, cols), BF)


def call(body, outs, scalars, arrays, scratch=(), limit=40, flops=0, later=()):
    count, skip = len(scalars) + len(arrays), len(later)

    def without(*refs):
        body(*refs[:count], *refs[count + skip :])

    return pl.pallas_call(
        without,
        out_shape=outs,
        in_specs=[SM] * len(scalars) + [VM] * len(arrays) + [pl.BlockSpec(memory_space=pl.ANY)] * skip,
        out_specs=[VM] * len(outs),
        scratch_shapes=list(scratch),
        compiler_params=pltpu.CompilerParams(vmem_limit_bytes=limit << 20),
        cost_estimate=pl.CostEstimate(flops=flops, bytes_accessed=1 << 20, transcendentals=0),
    )(*scalars, *arrays, *later)


def x_shift(value, k):
    return lax.ppermute(value, "dev", [(i, (i // 8) * 8 + (i + 2 * k) % 8) for i in range(32)])


def z_shift(value, k):
    return lax.ppermute(value, "dev", [(i, (i + 8 * k) % 32) for i in range(32)])


def z_trade(value):
    groups = [[z * 8 + i for z in range(RING)] for i in range(8)]
    return lax.all_to_all(value, "dev", 0, 0, tiled=True, axis_index_groups=groups)


def core_swap(value):
    return lax.ppermute(value, "dev", [(i, i ^ 1) for i in range(32)])


def aligned(value, unit):
    return pl.multiple_of(value * unit, unit)


def split_tile_body(pos, tile, *outs):
    for k in range(RING):
        outs[k][...] = tile[pl.ds(aligned((pos[1] + k) % RING, 64), 64), :]


def pack_body(pos, *refs):
    ins, outs = refs[:RING], refs[RING:]
    for k in range(RING):
        for j in range(RING):
            outs[k][16 * j : 16 * j + 16, :] = ins[j][pl.ds(aligned((pos[0] + k) % RING, 16), 16), :]


def first_of(tpi, image):
    row, col = image // IMG_G, image % IMG_G
    total = jnp.int32(0)
    for j in range(IMG_G):
        total = total + jnp.where(j < col, tpi[row * IMG_G + j], 0)
    return total


def select_body(pos, tpi, table, *refs):
    ins, out, held = refs[:RING], refs[RING], refs[RING + 1]
    for k in range(RING):
        held[64 * k : 64 * k + 64, :] = ins[k][...]
    for item in range(8 * SLOTS):
        first = first_of(tpi, table[item])
        for u in range(2):
            step = ((pos[2] + first) & 1) + 2 * u
            chip = jnp.minimum(first + step, 31) // 2
            zk = (pos[0] - chip // RING + RING) % RING
            xk = (pos[1] - chip % RING + RING) % RING
            row = (item * 2 + u) * 16
            out[row : row + 16, :] = held[pl.ds(aligned(zk * RING + xk, 16), 16), :]


def pick_body(table, pos, received, *refs):
    refs[-1][...] = received[...]


def pick(pos, table, received, later):
    def index(i, table, pos):
        return ((table[pos[3] * SLOTS + i // 2] // IMG_G) * RING + i, 0)

    return pl.pallas_call(
        pick_body,
        out_shape=shape(RING * 16, DV),
        grid_spec=pltpu.PrefetchScalarGridSpec(
            num_scalar_prefetch=2,
            grid=(RING,),
            in_specs=[pl.BlockSpec((16, DV), index)] + [pl.BlockSpec(memory_space=pl.ANY)] * len(later),
            out_specs=pl.BlockSpec((16, DV), lambda i, table, pos: (i, 0)),
        ),
    )(table, pos, received, *later)


def join_body(*refs):
    size = refs[0].shape[0]
    for k in range(RING):
        refs[RING][k * size : (k + 1) * size, :] = refs[k][...]


def join(values, later=()):
    rows, cols = values[0].shape
    return call(join_body, [shape(RING * rows, cols)], (), tuple(values), later=later)[0]


def split_w_body(pos, w, mine, theirs):
    first = pos[2] == 0
    for p in range(RING):
        for j in range(3):
            at = j * DV + p * 2 * HALF
            lo, hi = w[:, at : at + HALF], w[:, at + HALF : at + 2 * HALF]
            mine[p, :, j * HALF : (j + 1) * HALF] = jnp.where(first, lo, hi)
            theirs[p, :, j * HALF : (j + 1) * HALF] = jnp.where(first, hi, lo)


def split_text_body(pos, kv, *outs):
    for k in range(RING):
        head = (pos[1] + k) % RING
        outs[k][:, :HD] = kv[:, pl.ds(aligned(head, HD), HD)]
        outs[k][:, HD:] = kv[:, pl.ds(aligned(head + KVH, HD), HD)]


def split_query_body(pos, query, *outs):
    for k in range(RING):
        outs[k][...] = query[:, pl.ds(aligned((pos[1] + k) % RING, GQ * HD), GQ * HD)]


def split_query(pos, query, later=()):
    return call(split_query_body, [shape(64, GQ * HD)] * RING, (pos,), (query,), later=later)


def assemble_rows(pos, blocks, tile):
    for k in range(RING):
        tile[pl.ds(aligned((pos[1] - k + RING) % RING, 64), 64), :] = blocks[k][...]


def weights_body(pos, *refs):
    for zk in range(RING):
        for xk in range(RING):
            row = ((pos[0] - zk + RING) % RING) * RING + (pos[1] - xk + RING) % RING
            refs[RING][pl.ds(aligned(row, 80), 80), :PART] = refs[zk][80 * xk : 80 * xk + 80, :]
    refs[RING][:, PART:] = jnp.zeros((DV, WIDE - PART), BF)


def encode_body(pos, gain, bias, *refs):
    blocks, held, out, tile = refs[:RING], refs[RING : RING + 2], refs[RING + 2], refs[RING + 3]
    assemble_rows(pos, blocks, tile)
    value = tile[...].astype(F32)
    center = jnp.mean(value, axis=-1, keepdims=True)
    value = value - center
    spread = jnp.mean(jnp.square(value), axis=-1, keepdims=True)
    normed = (value * lax.rsqrt(spread + 1e-05) * gain[...] + bias[...]).astype(BF)
    lane = lax.broadcasted_iota(jnp.int32, (TILE_ROWS, HALF), 1)
    scale = LOG2E / math.sqrt(VHD)
    for half in range(2):
        qkv = jnp.dot(normed, held[half][...], preferred_element_type=F32).astype(BF)
        query, key, value = qkv[:, :HALF], qkv[:, HALF : 2 * HALF], qkv[:, 2 * HALF : PART]
        context = jnp.zeros((TILE_ROWS, HALF), F32)
        for h in range(2):
            mine = (lane < VHD) == (h == 0)
            zero = jnp.zeros((), BF)
            scores = lax.dot_general(
                jnp.where(mine, query, zero), key, (((1,), (1,)), ((), ())), preferred_element_type=F32
            )
            highest = jnp.max(scores, axis=-1, keepdims=True)
            exponent = jnp.exp2((scores - highest) * scale)
            total = jnp.sum(exponent, axis=-1, keepdims=True)
            weight = (exponent / total).astype(BF)
            context = context + jnp.dot(weight, jnp.where(mine, value, zero), preferred_element_type=F32)
        out[:, half * HALF : (half + 1) * HALF] = context.astype(BF)


def project_body(pos, k_gain, w_out, w_kv, *refs):
    blocks, contexts = refs[:RING], refs[RING : 2 * RING]
    out, tile, held = refs[2 * RING :]
    assemble_rows(pos, blocks, tile)
    total = tile[...].astype(F32)
    for k in range(RING):
        part = (pos[1] - k + RING) % RING
        held[:HALF, :] = w_out[pl.ds(aligned(part * 2 + pos[2], HALF), HALF), :]
        held[HALF:, :] = w_out[pl.ds(aligned(part * 2 + 1 - pos[2], HALF), HALF), :]
        total = total + jnp.dot(contexts[k][...], held[...], preferred_element_type=F32)
    residual = total.astype(BF)
    key = jnp.dot(residual, w_kv[:, pl.ds(aligned(pos[1], HD), HD)], preferred_element_type=F32)
    value = jnp.dot(residual, w_kv[:, pl.ds(aligned(pos[1] + KVH, HD), HD)], preferred_element_type=F32)
    key = key * lax.rsqrt(jnp.mean(jnp.square(key), axis=-1, keepdims=True) + 1e-06) * k_gain[...]
    out[:, :HD] = key.astype(BF)
    out[:, HD:] = value.astype(BF)


BLOCK = 256
STACK = RING * GQ * 64


def softmax_rows(query, keys, values, seen):
    scores = lax.dot_general(query, keys, (((1,), (1,)), ((), ())), preferred_element_type=F32)
    scores = seen(scores)
    highest = jnp.max(scores, axis=-1, keepdims=True)
    exponent = jnp.exp2((scores - highest) * (LOG2E / math.sqrt(HD)))
    total = jnp.sum(exponent, axis=-1, keepdims=True)
    result = jnp.dot(exponent.astype(BF), values, preferred_element_type=F32)
    return (result / total).astype(BF)


def attend_rows(pos, queries, outs, held_q, held_o, held_k, held_v, seen_at):
    for k in range(RING):
        for h in range(GQ):
            held_q[(k * GQ + h) * 64 : (k * GQ + h + 1) * 64, :] = queries[k][:, h * HD : (h + 1) * HD]

    def block(i, carry):
        at = pl.ds(pl.multiple_of(i * BLOCK, BLOCK), BLOCK)
        source = (pos[1] - i // (GQ * 64 // BLOCK) + RING) % RING
        row = lax.broadcasted_iota(jnp.int32, (BLOCK, 1), 0) % 64
        seen = seen_at(source * 128 + pos[2] * 64 + row)
        held_o[at, :] = softmax_rows(held_q[at, :], held_k[...], held_v[...], seen)
        return carry

    lax.fori_loop(0, STACK // BLOCK, block, 0, unroll=8)
    for k in range(RING):
        for h in range(GQ):
            outs[k][:, h * HD : (h + 1) * HD] = held_o[(k * GQ + h) * 64 : (k * GQ + h + 1) * 64, :]


def cross_body(pos, tpi, table, offsets, *refs):
    queries, sides, outs = refs[:RING], refs[RING : RING + 2], refs[RING + 2 : 2 * RING + 2]
    held_q, held_o, held_k, held_v = refs[2 * RING + 2 :]
    for n in range(2):
        held_k[n * 1024 : (n + 1) * 1024, :] = sides[n][:, :HD]
        held_v[n * 1024 : (n + 1) * 1024, :] = sides[n][:, HD:]
    group = pos[3]
    slot_of, low_of = [], []
    images = [table[group * SLOTS + s] for s in range(SLOTS)]
    firsts = [first_of(tpi, image) for image in images]
    counts = [tpi[image] for image in images]
    for n in range(2 * RING):
        entry = (pos[0] - n % RING + RING) % RING
        slot, u = entry // 2, entry % 2
        core = pos[2] if n < RING else 1 - pos[2]
        first = jnp.where(slot == 0, firsts[0], firsts[1])
        count = jnp.where(slot == 0, counts[0], counts[1])
        step = ((core + first) & 1) + 2 * u
        slot_of.append(slot)
        low_of.append(jnp.where(step < count, 0.0, LOW).astype(F32))

    def seen_at(local):
        position = offsets[group] + pos[0] * 512 + local

        def seen(scores):
            parts = []
            for n in range(2 * RING):
                low = jnp.where(position >= slot_of[n] * SLOT_SPAN, low_of[n], LOW)
                parts.append(scores[:, n * TILE_ROWS : (n + 1) * TILE_ROWS] + low)
            return jnp.concatenate(parts, axis=1)

        return seen

    attend_rows(pos, queries, outs, held_q, held_o, held_k, held_v, seen_at)


def self_body(pos, *refs):
    queries, sides, outs = refs[:RING], refs[RING : RING + 2], refs[RING + 2 : 2 * RING + 2]
    held_q, held_o, held_k, held_v = refs[2 * RING + 2 :]
    for n in range(2):
        for k in range(RING):
            at = k * 512 + n * 256
            held_k[at : at + 256, :] = sides[n][k * 256 : (k + 1) * 256, :HD]
            held_v[at : at + 256, :] = sides[n][k * 256 : (k + 1) * 256, HD:]

    def seen_at(local):
        col = lax.broadcasted_iota(jnp.int32, (1, 512), 1)
        piece = col // 64
        core = jnp.where(piece < RING, pos[2], 1 - pos[2])
        key_at = (pos[1] - piece % RING + RING) % RING * 128 + core * 64 + col % 64

        def seen(scores):
            parts = [jnp.where(key_at <= local, scores[:, :512], LOW)]
            for k in range(1, RING):
                low = jnp.where(pos[0] >= k, 0.0, LOW).astype(F32)
                parts.append(scores[:, k * 512 : (k + 1) * 512] + low)
            return jnp.concatenate(parts, axis=1)

        return seen

    attend_rows(pos, queries, outs, held_q, held_o, held_k, held_v, seen_at)


def place_body(pos, *refs):
    ins, out = refs[:RING], refs[RING]
    for k in range(RING):
        out[:, pl.ds(aligned((pos[1] + k) % RING, GQ * HD), GQ * HD)] = ins[k][...]


def per_device(
    tiles,
    w_qkv,
    w_out,
    w_kv,
    ln_gain,
    ln_bias,
    k_gain,
    cross_queries,
    self_queries,
    text_kv,
    tiles_per_image,
    request_table,
    span_offsets,
):
    dev = lax.axis_index("dev")
    pos = jnp.stack([dev // 8, (dev // 2) % 4, dev % 2, lax.axis_index("group")]).astype(jnp.int32)
    tpi = tiles_per_image.reshape(-1)
    table = request_table.reshape(-1)
    tokens = cross_queries.shape[0]
    ring = (1, 2, 3)

    blocks = call(split_tile_body, [shape(64, DV)] * RING, (pos,), (tiles.reshape(TILE_ROWS, DV),))
    spread = [blocks[0]] + [x_shift(blocks[k], k) for k in ring]
    mine, theirs = call(
        split_w_body, [jax.ShapeDtypeStruct((RING, 40, PART), BF)] * 2, (pos,), (w_qkv,), later=(blocks[0],)
    )
    got = core_swap(theirs)
    even = pos[2] == 0
    pair = jnp.concatenate([jnp.where(even, mine, got), jnp.where(even, got, mine)], axis=1)
    parts = [lax.dynamic_index_in_dim(pair, (pos[1] + k) % RING, 0, keepdims=False) for k in range(RING)]
    parts = [parts[0]] + [x_shift(parts[k], k) for k in ring]

    packed = call(pack_body, [shape(64, DV)] * RING, (pos,), tuple(spread), later=(pair,))
    packed = [packed[0]] + [z_shift(packed[k], k) for k in ring]
    chosen = call(
        select_body,
        [shape(8 * 64, DV)],
        (pos, tpi, table),
        tuple(packed),
        [pltpu.VMEM((TILE_ROWS, DV), BF)],
        later=tuple(parts[1:]),
    )[0]
    received = lax.all_to_all(chosen.reshape(8, 64, DV), "group", 0, 0, tiled=True).reshape(8 * 64, DV)
    joined = join(parts, later=(chosen,))
    weights = [joined] + [z_shift(joined, k) for k in ring]
    heads = call(split_text_body, [shape(64, 2 * HD)] * RING, (pos,), (text_kv,), later=(chosen,))
    heads = [heads[0]] + [x_shift(heads[k], k) for k in ring]
    own = split_query(pos, self_queries, later=(chosen,))
    own = [own[0]] + [x_shift(own[k], k) for k in ring]
    asked = split_query(pos, cross_queries, later=(chosen,))
    asked = [asked[0]] + [x_shift(asked[k], k) for k in ring]

    rows = z_trade(pick(pos, table, received, (*heads[1:], *own[1:], *asked[1:])))
    half = call(weights_body, [shape(DV, WIDE)], (pos,), tuple(weights), later=(rows,))[0]
    blocks = [rows] + [x_shift(rows, k) for k in ring]

    text = join(heads, later=(half,))
    text = [text] + [z_shift(text, k) for k in ring]
    context = call(
        encode_body,
        [shape(TILE_ROWS, 2 * HALF)],
        (pos,),
        (ln_gain.reshape(1, DV), ln_bias.reshape(1, DV), *blocks, half, core_swap(half)),
        [pltpu.VMEM((TILE_ROWS, DV), BF)],
        flops=1 << 30,
    )[0]
    contexts = [context] + [x_shift(context, k) for k in ring]
    text = join(text, later=(context,))
    piece = call(
        project_body,
        [shape(TILE_ROWS, 2 * HD)],
        (pos,),
        (k_gain.reshape(1, HD), w_out, w_kv, *blocks, *contexts),
        [pltpu.VMEM((TILE_ROWS, DV), BF), pltpu.VMEM((2 * HALF, DV), BF)],
        flops=1 << 30,
        later=(text,),
    )[0]
    pieces = [piece] + [z_shift(piece, k) for k in ring]
    own = call(
        self_body,
        [shape(64, GQ * HD)] * RING,
        (pos,),
        (*own, text, core_swap(text)),
        [pltpu.VMEM((STACK, HD), BF)] * 4,
        flops=1 << 32,
        later=(piece,),
    )
    pieces = join(pieces, later=(own[0],))
    own = [own[0]] + [x_shift(own[k], RING - k) for k in ring]
    back = call(
        cross_body,
        [shape(64, GQ * HD)] * RING,
        (pos, tpi, table, span_offsets),
        (*asked, pieces, core_swap(pieces)),
        [pltpu.VMEM((STACK, HD), BF)] * 4,
        flops=1 << 32,
    )
    back = [back[0]] + [x_shift(back[k], RING - k) for k in ring]
    self_out = call(place_body, [shape(tokens, RING * GQ * HD)], (pos,), tuple(own), later=(back[0],))[0]
    cross_out = call(place_body, [shape(tokens, RING * GQ * HD)], (pos,), tuple(back))[0]
    return (cross_out, self_out)


def solution(mesh):
    in_specs = (
        P(("group", "dev"), None, None),
        P("dev", None),
        P(),
        P(),
        P(),
        P(),
        P(),
        P(("group", "dev"), None),
        P(("group", "dev"), None),
        P(("group", "dev"), None),
        P(),
        P(),
        P(),
    )
    out_specs = (P(("group", "dev"), None), P(("group", "dev"), None))
    return jax.shard_map(
        per_device, mesh=mesh, in_specs=in_specs, out_specs=out_specs, check_vma=False
    )
```

```python
import math

import jax
import jax.numpy as jnp
from jax import lax
from jax.experimental import pallas as pl
from jax.experimental.pallas import tpu as pltpu
from jax.sharding import PartitionSpec as P

RING = 4
VHD = 80
HD = 128
KVH = 4
GQ = 8
SLOTS = 2
IMG_G = 16
TILE_ROWS = 256
DV = 1280
PART = 480
WIDE = 512
HALF = 160
SLOT_SPAN = 1024
LOG2E = math.log2(math.e)
LOW = -1e30
BF = jnp.bfloat16
F32 = jnp.float32
VM = pl.BlockSpec(memory_space=pltpu.VMEM)
SM = pl.BlockSpec(memory_space=pltpu.SMEM)


def shape(rows, cols):
    return jax.ShapeDtypeStruct((rows, cols), BF)


def call(body, outs, scalars, arrays, scratch=(), limit=40, flops=0, later=()):
    count, skip = len(scalars) + len(arrays), len(later)

    def without(*refs):
        body(*refs[:count], *refs[count + skip :])

    return pl.pallas_call(
        without,
        out_shape=outs,
        in_specs=[SM] * len(scalars) + [VM] * len(arrays) + [pl.BlockSpec(memory_space=pl.ANY)] * skip,
        out_specs=[VM] * len(outs),
        scratch_shapes=list(scratch),
        compiler_params=pltpu.CompilerParams(vmem_limit_bytes=limit << 20),
        cost_estimate=pl.CostEstimate(flops=flops, bytes_accessed=1 << 20, transcendentals=0),
    )(*scalars, *arrays, *later)


def x_shift(value, k):
    return lax.ppermute(value, "dev", [(i, (i // 8) * 8 + (i + 2 * k) % 8) for i in range(32)])


def z_shift(value, k):
    return lax.ppermute(value, "dev", [(i, (i + 8 * k) % 32) for i in range(32)])


def chip_trade(value):
    groups = [[chip * 2 + c for chip in range(RING * RING)] for c in range(2)]
    return lax.all_to_all(value, "dev", 0, 0, tiled=True, axis_index_groups=groups)


def z_trade(value):
    groups = [[z * 8 + i for z in range(RING)] for i in range(8)]
    return lax.all_to_all(value, "dev", 0, 0, tiled=True, axis_index_groups=groups)


def core_swap(value):
    return lax.ppermute(value, "dev", [(i, i ^ 1) for i in range(32)])


def aligned(value, unit):
    return pl.multiple_of(value * unit, unit)


def first_of(tpi, image):
    row, col = image // IMG_G, image % IMG_G
    total = jnp.int32(0)
    for j in range(IMG_G):
        total = total + jnp.where(j < col, tpi[row * IMG_G + j], 0)
    return total


def select_body(pos, tpi, table, held, out):
    for item in range(8 * SLOTS):
        first = first_of(tpi, table[item])
        for u in range(2):
            step = ((pos[2] + first) & 1) + 2 * u
            chip = jnp.minimum(first + step, 31) // 2
            row = (item * 2 + u) * 16
            out[row : row + 16, :] = held[pl.ds(aligned(chip, 16), 16), :]


def pick_body(pos, table, received, out, sems):
    copies = []
    for z in range(RING):
        owner = table[pos[3] * SLOTS + z // 2] // IMG_G
        source = received.at[pl.ds(aligned(owner * RING + z, 16), 16), :]
        copies.append(pltpu.make_async_copy(source, out.at[16 * z : 16 * z + 16, :], sems.at[z]))
    for copy in copies:
        copy.start()
    for copy in copies:
        copy.wait()


def pick(pos, table, received, later):
    def without(*refs):
        pick_body(*refs[:3], *refs[3 + len(later) :])

    return pl.pallas_call(
        without,
        out_shape=shape(RING * 16, DV),
        in_specs=[SM, SM] + [pl.BlockSpec(memory_space=pl.ANY)] * (1 + len(later)),
        out_specs=VM,
        scratch_shapes=[pltpu.SemaphoreType.DMA((RING,))],
    )(pos, table, received, *later)


def join_body(*refs):
    size = refs[0].shape[0]
    for k in range(RING):
        refs[RING][k * size : (k + 1) * size, :] = refs[k][...]


def join(values, later=()):
    rows, cols = values[0].shape
    return call(join_body, [shape(RING * rows, cols)], (), tuple(values), later=later)[0]


def split_w_body(pos, w, mine, theirs):
    first = pos[2] == 0
    for p in range(RING):
        for j in range(3):
            at = j * DV + p * 2 * HALF
            lo, hi = w[:, at : at + HALF], w[:, at + HALF : at + 2 * HALF]
            mine[p, :, j * HALF : (j + 1) * HALF] = jnp.where(first, lo, hi)
            theirs[p, :, j * HALF : (j + 1) * HALF] = jnp.where(first, hi, lo)


Q_COLS = GQ * HD
KV_AT = 2 * Q_COLS
PACK_COLS = KV_AT + 2 * HD


def pack_heads_body(pos, own, asked, text, *outs):
    for k in range(RING):
        head = (pos[1] + k) % RING
        outs[k][:, :Q_COLS] = own[:, pl.ds(aligned(head, Q_COLS), Q_COLS)]
        outs[k][:, Q_COLS:KV_AT] = asked[:, pl.ds(aligned(head, Q_COLS), Q_COLS)]
        outs[k][:, KV_AT : KV_AT + HD] = text[:, pl.ds(aligned(head, HD), HD)]
        outs[k][:, KV_AT + HD :] = text[:, pl.ds(aligned(head + KVH, HD), HD)]


def join_text_body(*refs):
    for k in range(RING):
        refs[RING][k * 64 : (k + 1) * 64, :] = refs[k][:, KV_AT:]


def assemble_rows(pos, blocks, tile):
    for k in range(RING):
        tile[pl.ds(aligned((pos[1] - k + RING) % RING, 64), 64), :] = blocks[k][...]


def weights_body(pos, mine, back, ahead, far_a, far_b, out):
    for zk, refs in ((0, (mine,)), (1, (back,)), (3, (ahead,)), (2, (far_a, far_b))):
        for xk in range(RING):
            row = ((pos[0] - zk + RING) % RING) * RING + (pos[1] - xk + RING) % RING
            ref = refs[xk * len(refs) // RING]
            at = 80 * xk if len(refs) == 1 else 80 * (xk % 2)
            out[pl.ds(aligned(row, 80), 80), :PART] = ref[at : at + 80, :]
    out[:, PART:] = jnp.zeros((DV, WIDE - PART), BF)


def encode_body(pos, gain, bias, *refs):
    blocks, held, out, tile = refs[:RING], refs[RING : RING + 2], refs[RING + 2], refs[RING + 3]
    assemble_rows(pos, blocks, tile)
    value = tile[...].astype(F32)
    center = jnp.mean(value, axis=-1, keepdims=True)
    value = value - center
    spread = jnp.mean(jnp.square(value), axis=-1, keepdims=True)
    normed = (value * lax.rsqrt(spread + 1e-05) * gain[...] + bias[...]).astype(BF)
    lane = lax.broadcasted_iota(jnp.int32, (TILE_ROWS, HALF), 1)
    scale = LOG2E / math.sqrt(VHD)
    for half in range(2):
        qkv = jnp.dot(normed, held[half][...], preferred_element_type=F32).astype(BF)
        query, key, value = qkv[:, :HALF], qkv[:, HALF : 2 * HALF], qkv[:, 2 * HALF : PART]
        context = jnp.zeros((TILE_ROWS, HALF), F32)
        for h in range(2):
            mine = (lane < VHD) == (h == 0)
            zero = jnp.zeros((), BF)
            scores = lax.dot_general(
                jnp.where(mine, query, zero), key, (((1,), (1,)), ((), ())), preferred_element_type=F32
            )
            highest = jnp.max(scores, axis=-1, keepdims=True)
            exponent = jnp.exp2((scores - highest) * scale)
            total = jnp.sum(exponent, axis=-1, keepdims=True)
            weight = (exponent / total).astype(BF)
            context = context + jnp.dot(weight, jnp.where(mine, value, zero), preferred_element_type=F32)
        out[:, half * HALF : (half + 1) * HALF] = context.astype(BF)


def project_body(pos, k_gain, w_out, w_kv, *refs):
    blocks, contexts = refs[:RING], refs[RING : 2 * RING]
    out, tile, held = refs[2 * RING :]
    assemble_rows(pos, blocks, tile)
    total = tile[...].astype(F32)
    for k in range(RING):
        part = (pos[1] - k + RING) % RING
        held[:HALF, :] = w_out[pl.ds(aligned(part * 2 + pos[2], HALF), HALF), :]
        held[HALF:, :] = w_out[pl.ds(aligned(part * 2 + 1 - pos[2], HALF), HALF), :]
        total = total + jnp.dot(contexts[k][...], held[...], preferred_element_type=F32)
    residual = total.astype(BF)
    key = jnp.dot(residual, w_kv[:, pl.ds(aligned(pos[1], HD), HD)], preferred_element_type=F32)
    value = jnp.dot(residual, w_kv[:, pl.ds(aligned(pos[1] + KVH, HD), HD)], preferred_element_type=F32)
    key = key * lax.rsqrt(jnp.mean(jnp.square(key), axis=-1, keepdims=True) + 1e-06) * k_gain[...]
    out[:, :HD] = key.astype(BF)
    out[:, HD:] = value.astype(BF)


BLOCK = 256
STACK = RING * GQ * 64


def softmax_rows(query, keys, values, seen):
    scores = lax.dot_general(query, keys, (((1,), (1,)), ((), ())), preferred_element_type=F32)
    scores = seen(scores)
    highest = jnp.max(scores, axis=-1, keepdims=True)
    exponent = jnp.exp2((scores - highest) * (LOG2E / math.sqrt(HD)))
    total = jnp.sum(exponent, axis=-1, keepdims=True)
    result = jnp.dot(exponent.astype(BF), values, preferred_element_type=F32)
    return (result / total).astype(BF)


def attend_rows(pos, packed, column, outs, held_q, held_o, held_k, held_v, seen_at):
    for k in range(RING):
        for h in range(GQ):
            lane = column + h * HD
            held_q[(k * GQ + h) * 64 : (k * GQ + h + 1) * 64, :] = packed[k][:, lane : lane + HD]

    def block(i, carry):
        at = pl.ds(pl.multiple_of(i * BLOCK, BLOCK), BLOCK)
        source = (pos[1] - i // (GQ * 64 // BLOCK) + RING) % RING
        row = lax.broadcasted_iota(jnp.int32, (BLOCK, 1), 0) % 64
        seen = seen_at(source * 128 + pos[2] * 64 + row)
        held_o[at, :] = softmax_rows(held_q[at, :], held_k[...], held_v[...], seen)
        return carry

    lax.fori_loop(0, STACK // BLOCK, block, 0, unroll=8)
    for k in range(RING):
        for h in range(GQ):
            outs[k][:, h * HD : (h + 1) * HD] = held_o[(k * GQ + h) * 64 : (k * GQ + h + 1) * 64, :]


def cross_body(pos, tpi, table, offsets, *refs):
    queries, sides, outs = refs[:RING], refs[RING : RING + 2], refs[RING + 2 : 2 * RING + 2]
    held_q, held_o, held_k, held_v = refs[2 * RING + 2 :]
    for n in range(2):
        held_k[n * 1024 : (n + 1) * 1024, :] = sides[n][:, :HD]
        held_v[n * 1024 : (n + 1) * 1024, :] = sides[n][:, HD:]
    group = pos[3]
    slot_of, low_of = [], []
    images = [table[group * SLOTS + s] for s in range(SLOTS)]
    firsts = [first_of(tpi, image) for image in images]
    counts = [tpi[image] for image in images]
    for n in range(2 * RING):
        entry = (pos[0] - n % RING + RING) % RING
        slot, u = entry // 2, entry % 2
        core = pos[2] if n < RING else 1 - pos[2]
        first = jnp.where(slot == 0, firsts[0], firsts[1])
        count = jnp.where(slot == 0, counts[0], counts[1])
        step = ((core + first) & 1) + 2 * u
        slot_of.append(slot)
        low_of.append(jnp.where(step < count, 0.0, LOW).astype(F32))

    def seen_at(local):
        position = offsets[group] + pos[0] * 512 + local

        def seen(scores):
            parts = []
            for n in range(2 * RING):
                low = jnp.where(position >= slot_of[n] * SLOT_SPAN, low_of[n], LOW)
                parts.append(scores[:, n * TILE_ROWS : (n + 1) * TILE_ROWS] + low)
            return jnp.concatenate(parts, axis=1)

        return seen

    attend_rows(pos, queries, Q_COLS, outs, held_q, held_o, held_k, held_v, seen_at)


def self_body(pos, *refs):
    queries, sides, outs = refs[:RING], refs[RING : RING + 2], refs[RING + 2 : 2 * RING + 2]
    held_q, held_o, held_k, held_v = refs[2 * RING + 2 :]
    for n in range(2):
        for k in range(RING):
            at = k * 512 + n * 256
            held_k[at : at + 256, :] = sides[n][k * 256 : (k + 1) * 256, :HD]
            held_v[at : at + 256, :] = sides[n][k * 256 : (k + 1) * 256, HD:]

    def seen_at(local):
        col = lax.broadcasted_iota(jnp.int32, (1, 512), 1)
        piece = col // 64
        core = jnp.where(piece < RING, pos[2], 1 - pos[2])
        key_at = (pos[1] - piece % RING + RING) % RING * 128 + core * 64 + col % 64

        def seen(scores):
            parts = [jnp.where(key_at <= local, scores[:, :512], LOW)]
            for k in range(1, RING):
                low = jnp.where(pos[0] >= k, 0.0, LOW).astype(F32)
                parts.append(scores[:, k * 512 : (k + 1) * 512] + low)
            return jnp.concatenate(parts, axis=1)

        return seen

    attend_rows(pos, queries, 0, outs, held_q, held_o, held_k, held_v, seen_at)


def place_body(pos, *refs):
    ins, out = refs[:RING], refs[RING]
    for k in range(RING):
        out[:, pl.ds(aligned((pos[1] + k) % RING, GQ * HD), GQ * HD)] = ins[k][...]


def per_device(
    tiles,
    w_qkv,
    w_out,
    w_kv,
    ln_gain,
    ln_bias,
    k_gain,
    cross_queries,
    self_queries,
    text_kv,
    tiles_per_image,
    request_table,
    span_offsets,
):
    dev = lax.axis_index("dev")
    pos = jnp.stack([dev // 8, (dev // 2) % 4, dev % 2, lax.axis_index("group")]).astype(jnp.int32)
    tpi = tiles_per_image.reshape(-1)
    table = request_table.reshape(-1)
    tokens = cross_queries.shape[0]
    ring = (1, 2, 3)

    held = chip_trade(tiles.reshape(TILE_ROWS, DV))
    mine, theirs = call(split_w_body, [jax.ShapeDtypeStruct((RING, 40, PART), BF)] * 2, (pos,), (w_qkv,))
    got = core_swap(theirs)
    even = pos[2] == 0
    pair = jnp.concatenate([jnp.where(even, mine, got), jnp.where(even, got, mine)], axis=1)
    parts = [lax.dynamic_index_in_dim(pair, (pos[1] + k) % RING, 0, keepdims=False) for k in range(RING)]
    parts = [parts[0]] + [x_shift(parts[k], k) for k in ring]
    chosen = call(
        select_body, [shape(8 * 64, DV)], (pos, tpi, table), (held,), later=tuple(parts[1:])
    )[0]

    received = lax.all_to_all(chosen.reshape(8, 64, DV), "group", 0, 0, tiled=True).reshape(8 * 64, DV)
    joined = join(parts, later=(chosen,))
    back, ahead = z_shift(joined, 1), z_shift(joined, 3)
    weights = (joined, back, ahead, z_shift(back[:160], 1), z_shift(ahead[160:], 3))

    heads = call(
        pack_heads_body,
        [shape(64, PACK_COLS)] * RING,
        (pos,),
        (self_queries, cross_queries, text_kv),
        later=(chosen,),
    )
    heads = [heads[0]] + [x_shift(heads[k], k) for k in ring]
    rows = z_trade(pick(pos, table, received, tuple(heads[1:])))
    blocks = [rows] + [x_shift(rows, k) for k in ring]
    half = call(weights_body, [shape(DV, WIDE)], (pos,), weights, later=(rows,))[0]

    text = call(join_text_body, [shape(TILE_ROWS, 2 * HD)], (), tuple(heads), later=(half,))[0]
    text = [text] + [z_shift(text, k) for k in ring]
    context = call(
        encode_body,
        [shape(TILE_ROWS, 2 * HALF)],
        (pos,),
        (ln_gain.reshape(1, DV), ln_bias.reshape(1, DV), *blocks, half, core_swap(half)),
        [pltpu.VMEM((TILE_ROWS, DV), BF)],
        flops=1 << 30,
    )[0]
    contexts = [context] + [x_shift(context, k) for k in ring]
    piece = call(
        project_body,
        [shape(TILE_ROWS, 2 * HD)],
        (pos,),
        (k_gain.reshape(1, HD), w_out, w_kv, *blocks, *contexts),
        [pltpu.VMEM((TILE_ROWS, DV), BF), pltpu.VMEM((2 * HALF, DV), BF)],
        flops=1 << 30,
        later=tuple(text[1:]),
    )[0]
    pieces = [piece] + [z_shift(piece, k) for k in ring]
    text = join(text, later=(piece,))
    own = call(
        self_body,
        [shape(64, Q_COLS)] * RING,
        (pos,),
        (*heads, text, core_swap(text)),
        [pltpu.VMEM((STACK, HD), BF)] * 4,
        flops=1 << 32,
        later=(piece,),
    )
    pieces = join(pieces, later=(own[0],))
    own = [own[0]] + [x_shift(own[k], RING - k) for k in ring]
    back = call(
        cross_body,
        [shape(64, Q_COLS)] * RING,
        (pos, tpi, table, span_offsets),
        (*heads, pieces, core_swap(pieces)),
        [pltpu.VMEM((STACK, HD), BF)] * 4,
        flops=1 << 32,
    )
    back = [back[0]] + [x_shift(back[k], RING - k) for k in ring]
    self_out = call(place_body, [shape(tokens, RING * Q_COLS)], (pos,), tuple(own), later=(back[0],))[0]
    cross_out = call(place_body, [shape(tokens, RING * Q_COLS)], (pos,), tuple(back))[0]
    return (cross_out, self_out)


def solution(mesh):
    in_specs = (
        P(("group", "dev"), None, None),
        P("dev", None),
        P(),
        P(),
        P(),
        P(),
        P(),
        P(("group", "dev"), None),
        P(("group", "dev"), None),
        P(("group", "dev"), None),
        P(),
        P(),
        P(),
    )
    out_specs = (P(("group", "dev"), None), P(("group", "dev"), None))
    return jax.shard_map(
        per_device, mesh=mesh, in_specs=in_specs, out_specs=out_specs, check_vma=False
    )
```

```python
import math

import jax
import jax.numpy as jnp
from jax import lax
from jax.experimental import pallas as pl
from jax.experimental.pallas import tpu as pltpu
from jax.sharding import PartitionSpec as P

RING = 4
VHD = 80
HD = 128
KVH = 4
GQ = 8
SLOTS = 2
IMG_G = 16
TILE_ROWS = 256
DV = 1280
PART = 480
WIDE = 512
HALF = 160
SLOT_SPAN = 1024
LOG2E = math.log2(math.e)
LOW = -1e30
BF = jnp.bfloat16
F32 = jnp.float32
VM = pl.BlockSpec(memory_space=pltpu.VMEM)
SM = pl.BlockSpec(memory_space=pltpu.SMEM)


def shape(rows, cols):
    return jax.ShapeDtypeStruct((rows, cols), BF)


def call(body, outs, scalars, arrays, scratch=(), limit=40, flops=0, later=()):
    count, skip = len(scalars) + len(arrays), len(later)

    def without(*refs):
        body(*refs[:count], *refs[count + skip :])

    return pl.pallas_call(
        without,
        out_shape=outs,
        in_specs=[SM] * len(scalars) + [VM] * len(arrays) + [pl.BlockSpec(memory_space=pl.ANY)] * skip,
        out_specs=[VM] * len(outs),
        scratch_shapes=list(scratch),
        compiler_params=pltpu.CompilerParams(vmem_limit_bytes=limit << 20),
        cost_estimate=pl.CostEstimate(flops=flops, bytes_accessed=1 << 20, transcendentals=0),
    )(*scalars, *arrays, *later)


def x_shift(value, k):
    return lax.ppermute(value, "dev", [(i, (i // 8) * 8 + (i + 2 * k) % 8) for i in range(32)])


def z_shift(value, k):
    return lax.ppermute(value, "dev", [(i, (i + 8 * k) % 32) for i in range(32)])


def chip_trade(value):
    groups = [[chip * 2 + c for chip in range(RING * RING)] for c in range(2)]
    return lax.all_to_all(value, "dev", 0, 0, tiled=True, axis_index_groups=groups)


def z_trade(value):
    groups = [[z * 8 + i for z in range(RING)] for i in range(8)]
    return lax.all_to_all(value, "dev", 0, 0, tiled=True, axis_index_groups=groups)


def core_swap(value):
    return lax.ppermute(value, "dev", [(i, i ^ 1) for i in range(32)])


def aligned(value, unit):
    return pl.multiple_of(value * unit, unit)


def first_of(tpi, image):
    row, col = image // IMG_G, image % IMG_G
    total = jnp.int32(0)
    for j in range(IMG_G):
        total = total + jnp.where(j < col, tpi[row * IMG_G + j], 0)
    return total


def select_body(pos, tpi, table, held, out):
    for item in range(8 * SLOTS):
        first = first_of(tpi, table[item])
        for u in range(2):
            step = ((pos[2] + first) & 1) + 2 * u
            chip = jnp.minimum(first + step, 31) // 2
            row = (item * 2 + u) * 16
            out[row : row + 16, :] = held[pl.ds(aligned(chip, 16), 16), :]


def pick_body(pos, table, received, out, sems):
    copies = []
    for z in range(RING):
        owner = table[pos[3] * SLOTS + z // 2] // IMG_G
        source = received.at[pl.ds(aligned(owner * RING + z, 16), 16), :]
        copies.append(pltpu.make_async_copy(source, out.at[16 * z : 16 * z + 16, :], sems.at[z]))
    for copy in copies:
        copy.start()
    for copy in copies:
        copy.wait()


def pick(pos, table, received, later):
    def without(*refs):
        pick_body(*refs[:3], *refs[3 + len(later) :])

    return pl.pallas_call(
        without,
        out_shape=shape(RING * 16, DV),
        in_specs=[SM, SM] + [pl.BlockSpec(memory_space=pl.ANY)] * (1 + len(later)),
        out_specs=VM,
        scratch_shapes=[pltpu.SemaphoreType.DMA((RING,))],
    )(pos, table, received, *later)


def join_body(*refs):
    size = refs[0].shape[0]
    for k in range(RING):
        refs[RING][k * size : (k + 1) * size, :] = refs[k][...]


def join(values, later=()):
    rows, cols = values[0].shape
    return call(join_body, [shape(RING * rows, cols)], (), tuple(values), later=later)[0]


def split_w_body(pos, w, mine, theirs):
    first = pos[2] == 0
    for p in range(RING):
        for j in range(3):
            at = j * DV + p * 2 * HALF
            lo, hi = w[:, at : at + HALF], w[:, at + HALF : at + 2 * HALF]
            mine[p, :, j * HALF : (j + 1) * HALF] = jnp.where(first, lo, hi)
            theirs[p, :, j * HALF : (j + 1) * HALF] = jnp.where(first, hi, lo)


Q_COLS = GQ * HD
KV_AT = 2 * Q_COLS
PACK_COLS = KV_AT + 2 * HD


def pack_heads_body(pos, own, asked, text, *outs):
    for k in range(RING):
        head = (pos[1] + k) % RING
        outs[k][:, :Q_COLS] = own[:, pl.ds(aligned(head, Q_COLS), Q_COLS)]
        outs[k][:, Q_COLS:KV_AT] = asked[:, pl.ds(aligned(head, Q_COLS), Q_COLS)]
        outs[k][:, KV_AT : KV_AT + HD] = text[:, pl.ds(aligned(head, HD), HD)]
        outs[k][:, KV_AT + HD :] = text[:, pl.ds(aligned(head + KVH, HD), HD)]


def join_text_body(*refs):
    for k in range(RING):
        refs[RING][k * 64 : (k + 1) * 64, :] = refs[k][:, KV_AT:]


def assemble_rows(pos, blocks, tile):
    for k in range(RING):
        tile[pl.ds(aligned((pos[1] - k + RING) % RING, 64), 64), :] = blocks[k][...]


def weights_body(pos, mine, back, ahead, far_a, far_b, out):
    for zk, refs in ((0, (mine,)), (1, (back,)), (3, (ahead,)), (2, (far_a, far_b))):
        for xk in range(RING):
            row = ((pos[0] - zk + RING) % RING) * RING + (pos[1] - xk + RING) % RING
            ref = refs[xk * len(refs) // RING]
            at = 80 * xk if len(refs) == 1 else 80 * (xk % 2)
            out[pl.ds(aligned(row, 80), 80), :PART] = ref[at : at + 80, :]
    out[:, PART:] = jnp.zeros((DV, WIDE - PART), BF)


def encode_body(pos, gain, bias, *refs):
    blocks, held, out, tile = refs[:RING], refs[RING : RING + 2], refs[RING + 2], refs[RING + 3]
    assemble_rows(pos, blocks, tile)
    value = tile[...].astype(F32)
    center = jnp.mean(value, axis=-1, keepdims=True)
    value = value - center
    spread = jnp.mean(jnp.square(value), axis=-1, keepdims=True)
    normed = (value * lax.rsqrt(spread + 1e-05) * gain[...] + bias[...]).astype(BF)
    lane = lax.broadcasted_iota(jnp.int32, (TILE_ROWS, HALF), 1)
    scale = LOG2E / math.sqrt(VHD)
    for half in range(2):
        qkv = jnp.dot(normed, held[half][...], preferred_element_type=F32).astype(BF)
        query, key, value = qkv[:, :HALF], qkv[:, HALF : 2 * HALF], qkv[:, 2 * HALF : PART]
        context = jnp.zeros((TILE_ROWS, HALF), F32)
        for h in range(2):
            mine = (lane < VHD) == (h == 0)
            zero = jnp.zeros((), BF)
            scores = lax.dot_general(
                jnp.where(mine, query, zero), key, (((1,), (1,)), ((), ())), preferred_element_type=F32
            )
            highest = jnp.max(scores, axis=-1, keepdims=True)
            exponent = jnp.exp2((scores - highest) * scale)
            total = jnp.sum(exponent, axis=-1, keepdims=True)
            weight = (exponent / total).astype(BF)
            context = context + jnp.dot(weight, jnp.where(mine, value, zero), preferred_element_type=F32)
        out[:, half * HALF : (half + 1) * HALF] = context.astype(BF)


def project_body(pos, k_gain, w_out, w_kv, *refs):
    blocks, contexts = refs[:RING], refs[RING : 2 * RING]
    out, tile, held = refs[2 * RING :]
    assemble_rows(pos, blocks, tile)
    total = tile[...].astype(F32)
    for k in range(RING):
        part = (pos[1] - k + RING) % RING
        held[:HALF, :] = w_out[pl.ds(aligned(part * 2 + pos[2], HALF), HALF), :]
        held[HALF:, :] = w_out[pl.ds(aligned(part * 2 + 1 - pos[2], HALF), HALF), :]
        total = total + jnp.dot(contexts[k][...], held[...], preferred_element_type=F32)
    residual = total.astype(BF)
    key = jnp.dot(residual, w_kv[:, pl.ds(aligned(pos[1], HD), HD)], preferred_element_type=F32)
    value = jnp.dot(residual, w_kv[:, pl.ds(aligned(pos[1] + KVH, HD), HD)], preferred_element_type=F32)
    key = key * lax.rsqrt(jnp.mean(jnp.square(key), axis=-1, keepdims=True) + 1e-06) * k_gain[...]
    out[:, :HD] = key.astype(BF)
    out[:, HD:] = value.astype(BF)


BLOCK = 256
STACK = RING * GQ * 64


def softmax_rows(query, keys, values, seen):
    scores = lax.dot_general(query, keys, (((1,), (1,)), ((), ())), preferred_element_type=F32)
    scores = seen(scores)
    highest = jnp.max(scores, axis=-1, keepdims=True)
    exponent = jnp.exp2((scores - highest) * (LOG2E / math.sqrt(HD)))
    result = jnp.dot(exponent.astype(BF), values, preferred_element_type=F32)
    return (result[:, :HD] / result[:, HD:]).astype(BF)


def attend_rows(pos, packed, column, outs, held_q, held_o, held_k, held_v, seen_at):
    for k in range(RING):
        for h in range(GQ):
            lane = column + h * HD
            held_q[(k * GQ + h) * 64 : (k * GQ + h + 1) * 64, :HD] = packed[k][:, lane : lane + HD]

    def block(i, carry):
        at = pl.ds(pl.multiple_of(i * BLOCK, BLOCK), BLOCK)
        source = (pos[1] - i // (GQ * 64 // BLOCK) + RING) % RING
        row = lax.broadcasted_iota(jnp.int32, (BLOCK, 1), 0) % 64
        seen = seen_at(source * 128 + pos[2] * 64 + row)
        held_o[at, :] = softmax_rows(held_q[at, :], held_k[...], held_v[...], seen)
        return carry

    lax.fori_loop(0, STACK // BLOCK, block, 0, unroll=8)
    for k in range(RING):
        for h in range(GQ):
            outs[k][:, h * HD : (h + 1) * HD] = held_o[(k * GQ + h) * 64 : (k * GQ + h + 1) * 64, :]


def cross_body(pos, tpi, table, offsets, *refs):
    queries, sides, outs = refs[:RING], refs[RING : RING + 2], refs[RING + 2 : 2 * RING + 2]
    held_q, held_o, held_k, held_v = refs[2 * RING + 2 :]
    group = pos[3]
    images = [table[group * SLOTS + s] for s in range(SLOTS)]
    firsts = [first_of(tpi, image) for image in images]
    counts = [tpi[image] for image in images]
    held_v[:, HD:] = jnp.ones((STACK, HD), BF)
    lane = lax.broadcasted_iota(jnp.int32, (TILE_ROWS, HD), 1)
    for n in range(2 * RING):
        rows = slice(n * TILE_ROWS, (n + 1) * TILE_ROWS)
        side = slice(n % RING * TILE_ROWS, (n % RING + 1) * TILE_ROWS)
        held_k[rows, :HD] = sides[n // RING][side, :HD]
        held_v[rows, :HD] = sides[n // RING][side, HD:]
        entry = (pos[0] - n % RING + RING) % RING
        slot, u = entry // 2, entry % 2
        core = pos[2] if n < RING else 1 - pos[2]
        first = jnp.where(slot == 0, firsts[0], firsts[1])
        count = jnp.where(slot == 0, counts[0], counts[1])
        step = ((core + first) & 1) + 2 * u
        none = jnp.where(step < count, 0.0, LOW).astype(F32)
        late = jnp.where(slot == 0, 0.0, LOW).astype(F32)
        held_k[rows, HD:] = jnp.where(lane == 0, none, jnp.where(lane == 1, late, 0.0)).astype(BF)
    for k in range(RING):
        source = (pos[1] - k + RING) % RING
        row = lax.broadcasted_iota(jnp.int32, (64, HD), 0)
        column = lax.broadcasted_iota(jnp.int32, (64, HD), 1)
        position = offsets[group] + pos[0] * 512 + source * 128 + pos[2] * 64 + row
        before = jnp.where(position < SLOT_SPAN, 1.0, 0.0)
        extra = jnp.where(column == 0, 1.0, jnp.where(column == 1, before, 0.0)).astype(BF)
        for h in range(GQ):
            held_q[(k * GQ + h) * 64 : (k * GQ + h + 1) * 64, HD:] = extra
    attend_rows(pos, queries, Q_COLS, outs, held_q, held_o, held_k, held_v, lambda local: lambda scores: scores)


def self_body(pos, *refs):
    queries, sides, outs = refs[:RING], refs[RING : RING + 2], refs[RING + 2 : 2 * RING + 2]
    held_q, held_o, held_k, held_v = refs[2 * RING + 2 :]
    for n in range(2):
        for k in range(RING):
            at = k * 512 + n * 256
            held_k[at : at + 256, :] = sides[n][k * 256 : (k + 1) * 256, :HD]
            held_v[at : at + 256, :HD] = sides[n][k * 256 : (k + 1) * 256, HD:]
    held_v[:, HD:] = jnp.ones((STACK, HD), BF)

    def seen_at(local):
        col = lax.broadcasted_iota(jnp.int32, (1, 512), 1)
        piece = col // 64
        core = jnp.where(piece < RING, pos[2], 1 - pos[2])
        key_at = (pos[1] - piece % RING + RING) % RING * 128 + core * 64 + col % 64

        def seen(scores):
            parts = [jnp.where(key_at <= local, scores[:, :512], LOW)]
            for k in range(1, RING):
                low = jnp.where(pos[0] >= k, 0.0, LOW).astype(F32)
                parts.append(scores[:, k * 512 : (k + 1) * 512] + low)
            return jnp.concatenate(parts, axis=1)

        return seen

    attend_rows(pos, queries, 0, outs, held_q, held_o, held_k, held_v, seen_at)


def place_body(pos, *refs):
    ins, out = refs[:RING], refs[RING]
    for k in range(RING):
        out[:, pl.ds(aligned((pos[1] + k) % RING, GQ * HD), GQ * HD)] = ins[k][...]


def per_device(
    tiles,
    w_qkv,
    w_out,
    w_kv,
    ln_gain,
    ln_bias,
    k_gain,
    cross_queries,
    self_queries,
    text_kv,
    tiles_per_image,
    request_table,
    span_offsets,
):
    dev = lax.axis_index("dev")
    pos = jnp.stack([dev // 8, (dev // 2) % 4, dev % 2, lax.axis_index("group")]).astype(jnp.int32)
    tpi = tiles_per_image.reshape(-1)
    table = request_table.reshape(-1)
    tokens = cross_queries.shape[0]
    ring = (1, 2, 3)

    held = chip_trade(tiles.reshape(TILE_ROWS, DV))
    mine, theirs = call(split_w_body, [jax.ShapeDtypeStruct((RING, 40, PART), BF)] * 2, (pos,), (w_qkv,))
    got = core_swap(theirs)
    even = pos[2] == 0
    pair = jnp.concatenate([jnp.where(even, mine, got), jnp.where(even, got, mine)], axis=1)
    parts = [lax.dynamic_index_in_dim(pair, (pos[1] + k) % RING, 0, keepdims=False) for k in range(RING)]
    parts = [parts[0]] + [x_shift(parts[k], k) for k in ring]
    chosen = call(
        select_body, [shape(8 * 64, DV)], (pos, tpi, table), (held,), later=tuple(parts[1:])
    )[0]

    received = lax.all_to_all(chosen.reshape(8, 64, DV), "group", 0, 0, tiled=True).reshape(8 * 64, DV)
    joined = join(parts, later=(chosen,))
    back, ahead = z_shift(joined, 1), z_shift(joined, 3)
    weights = (joined, back, ahead, z_shift(back[:160], 1), z_shift(ahead[160:], 3))

    heads = call(
        pack_heads_body,
        [shape(64, PACK_COLS)] * RING,
        (pos,),
        (self_queries, cross_queries, text_kv),
        later=(chosen,),
    )
    heads = [heads[0]] + [x_shift(heads[k], k) for k in ring]
    rows = z_trade(pick(pos, table, received, tuple(heads[1:])))
    blocks = [rows] + [x_shift(rows, k) for k in ring]
    half = call(weights_body, [shape(DV, WIDE)], (pos,), weights, later=(rows,))[0]

    text = call(join_text_body, [shape(TILE_ROWS, 2 * HD)], (), tuple(heads), later=(half,))[0]
    text = [text] + [z_shift(text, k) for k in ring]
    context = call(
        encode_body,
        [shape(TILE_ROWS, 2 * HALF)],
        (pos,),
        (ln_gain.reshape(1, DV), ln_bias.reshape(1, DV), *blocks, half, core_swap(half)),
        [pltpu.VMEM((TILE_ROWS, DV), BF)],
        flops=1 << 30,
    )[0]
    contexts = [context] + [x_shift(context, k) for k in ring]
    piece = call(
        project_body,
        [shape(TILE_ROWS, 2 * HD)],
        (pos,),
        (k_gain.reshape(1, HD), w_out, w_kv, *blocks, *contexts),
        [pltpu.VMEM((TILE_ROWS, DV), BF), pltpu.VMEM((2 * HALF, DV), BF)],
        flops=1 << 30,
        later=tuple(text[1:]),
    )[0]
    pieces = [piece] + [z_shift(piece, k) for k in ring]
    text = join(text, later=(piece,))
    own = call(
        self_body,
        [shape(64, Q_COLS)] * RING,
        (pos,),
        (*heads, text, core_swap(text)),
        [pltpu.VMEM((STACK, HD), BF)] * 3 + [pltpu.VMEM((STACK, 2 * HD), BF)],
        flops=1 << 32,
        later=(piece,),
    )
    pieces = join(pieces, later=(own[0],))
    own = [own[0]] + [x_shift(own[k], RING - k) for k in ring]
    back = call(
        cross_body,
        [shape(64, Q_COLS)] * RING,
        (pos, tpi, table, span_offsets),
        (*heads, pieces, core_swap(pieces)),
        [pltpu.VMEM((STACK, 2 * HD), BF), pltpu.VMEM((STACK, HD), BF)] + [pltpu.VMEM((STACK, 2 * HD), BF)] * 2,
        flops=1 << 32,
    )
    back = [back[0]] + [x_shift(back[k], RING - k) for k in ring]
    self_out = call(place_body, [shape(tokens, RING * Q_COLS)], (pos,), tuple(own), later=(back[0],))[0]
    cross_out = call(place_body, [shape(tokens, RING * Q_COLS)], (pos,), tuple(back))[0]
    return (cross_out, self_out)


def solution(mesh):
    in_specs = (
        P(("group", "dev"), None, None),
        P("dev", None),
        P(),
        P(),
        P(),
        P(),
        P(),
        P(("group", "dev"), None),
        P(("group", "dev"), None),
        P(("group", "dev"), None),
        P(),
        P(),
        P(),
    )
    out_specs = (P(("group", "dev"), None), P(("group", "dev"), None))
    return jax.shard_map(
        per_device, mesh=mesh, in_specs=in_specs, out_specs=out_specs, check_vma=False
    )
```

```python
import math

import jax
import jax.numpy as jnp
from jax import lax
from jax.experimental import pallas as pl
from jax.experimental.pallas import tpu as pltpu
from jax.sharding import PartitionSpec as P

RING = 4
VHD = 80
HD = 128
KVH = 4
GQ = 8
SLOTS = 2
IMG_G = 16
TILE_ROWS = 256
DV = 1280
PART = 480
WIDE = 512
HALF = 160
SLOT_SPAN = 1024
LOG2E = math.log2(math.e)
LOW = -1e30
BF = jnp.bfloat16
F32 = jnp.float32
VM = pl.BlockSpec(memory_space=pltpu.VMEM)
SM = pl.BlockSpec(memory_space=pltpu.SMEM)


def shape(rows, cols):
    return jax.ShapeDtypeStruct((rows, cols), BF)


def call(body, outs, scalars, arrays, scratch=(), limit=40, flops=0, later=()):
    count, skip = len(scalars) + len(arrays), len(later)

    def without(*refs):
        body(*refs[:count], *refs[count + skip :])

    return pl.pallas_call(
        without,
        out_shape=outs,
        in_specs=[SM] * len(scalars) + [VM] * len(arrays) + [pl.BlockSpec(memory_space=pl.ANY)] * skip,
        out_specs=[VM] * len(outs),
        scratch_shapes=list(scratch),
        compiler_params=pltpu.CompilerParams(vmem_limit_bytes=limit << 20),
        cost_estimate=pl.CostEstimate(flops=flops, bytes_accessed=1 << 20, transcendentals=0),
    )(*scalars, *arrays, *later)


def x_shift(value, k):
    return lax.ppermute(value, "dev", [(i, (i // 8) * 8 + (i + 2 * k) % 8) for i in range(32)])


def z_shift(value, k):
    return lax.ppermute(value, "dev", [(i, (i + 8 * k) % 32) for i in range(32)])


def chip_trade(value):
    groups = [[chip * 2 + c for chip in range(RING * RING)] for c in range(2)]
    return lax.all_to_all(value, "dev", 0, 0, tiled=True, axis_index_groups=groups)


def z_trade(value):
    groups = [[z * 8 + i for z in range(RING)] for i in range(8)]
    return lax.all_to_all(value, "dev", 0, 0, tiled=True, axis_index_groups=groups)


def core_swap(value):
    return lax.ppermute(value, "dev", [(i, i ^ 1) for i in range(32)])


def aligned(value, unit):
    return pl.multiple_of(value * unit, unit)


def first_of(tpi, image):
    row, col = image // IMG_G, image % IMG_G
    total = jnp.int32(0)
    for j in range(IMG_G):
        total = total + jnp.where(j < col, tpi[row * IMG_G + j], 0)
    return total


def select_body(pos, tpi, table, held, out):
    for item in range(8 * SLOTS):
        first = first_of(tpi, table[item])
        for u in range(2):
            step = ((pos[2] + first) & 1) + 2 * u
            chip = jnp.minimum(first + step, 31) // 2
            row = (item * 2 + u) * 16
            out[row : row + 16, :] = held[pl.ds(aligned(chip, 16), 16), :]


def pick_body(pos, table, received, out, sems):
    copies = []
    for z in range(RING):
        owner = table[pos[3] * SLOTS + z // 2] // IMG_G
        source = received.at[pl.ds(aligned(owner * RING + z, 16), 16), :]
        copies.append(pltpu.make_async_copy(source, out.at[16 * z : 16 * z + 16, :], sems.at[z]))
    for copy in copies:
        copy.start()
    for copy in copies:
        copy.wait()


def pick(pos, table, received, later):
    def without(*refs):
        pick_body(*refs[:3], *refs[3 + len(later) :])

    return pl.pallas_call(
        without,
        out_shape=shape(RING * 16, DV),
        in_specs=[SM, SM] + [pl.BlockSpec(memory_space=pl.ANY)] * (1 + len(later)),
        out_specs=VM,
        scratch_shapes=[pltpu.SemaphoreType.DMA((RING,))],
    )(pos, table, received, *later)


def join_body(*refs):
    size = refs[0].shape[0]
    for k in range(RING):
        refs[RING][k * size : (k + 1) * size, :] = refs[k][...]


def join(values, later=()):
    rows, cols = values[0].shape
    return call(join_body, [shape(RING * rows, cols)], (), tuple(values), later=later)[0]


def split_w_body(pos, w, mine, theirs):
    first = pos[2] == 0
    for p in range(RING):
        for j in range(3):
            at = j * DV + p * 2 * HALF
            lo, hi = w[:, at : at + HALF], w[:, at + HALF : at + 2 * HALF]
            mine[p, :, j * HALF : (j + 1) * HALF] = jnp.where(first, lo, hi)
            theirs[p, :, j * HALF : (j + 1) * HALF] = jnp.where(first, hi, lo)


Q_COLS = GQ * HD
KV_AT = 2 * Q_COLS
TEXT_ROWS = 32
PART_ROWS = 80 + TEXT_ROWS


def pack_parts_body(pos, pair, text, *outs):
    for k in range(RING):
        head = (pos[1] + k) % RING
        outs[k][:80, :PART] = pair[head]
        outs[k][:80, PART:] = jnp.zeros((80, WIDE - PART), BF)
        for n in range(2):
            rows, at = slice(n * TEXT_ROWS, (n + 1) * TEXT_ROWS), n * 2 * HD
            outs[k][80:, at : at + HD] = text[rows, pl.ds(aligned(head, HD), HD)]
            outs[k][80:, at + HD : at + 2 * HD] = text[rows, pl.ds(aligned(head + KVH, HD), HD)]


def pack_heads_body(pos, own, asked, *outs):
    for k in range(RING):
        head = (pos[1] + k) % RING
        outs[k][:, :Q_COLS] = own[:, pl.ds(aligned(head, Q_COLS), Q_COLS)]
        outs[k][:, Q_COLS:] = asked[:, pl.ds(aligned(head, Q_COLS), Q_COLS)]


def assemble_rows(pos, blocks, tile):
    for k in range(RING):
        tile[pl.ds(aligned((pos[1] - k + RING) % RING, 64), 64), :] = blocks[k][...]


def weights_body(pos, mine, back, ahead, far_a, far_b, out):
    for zk, refs in ((0, (mine,)), (1, (back,)), (3, (ahead,)), (2, (far_a, far_b))):
        for xk in range(RING):
            row = ((pos[0] - zk + RING) % RING) * RING + (pos[1] - xk + RING) % RING
            ref = refs[xk * len(refs) // RING]
            at = PART_ROWS * (xk if len(refs) == 1 else xk % 2)
            out[pl.ds(aligned(row, 80), 80), :] = ref[at : at + 80, :]
            for n in range(2):
                to, lane = DV + zk % 2 * 256 + xk * 64 + n * TEXT_ROWS, zk // 2 * 2 * HD
                out[to : to + TEXT_ROWS, lane : lane + 2 * HD] = ref[
                    at + 80 : at + PART_ROWS, n * 2 * HD : (n + 1) * 2 * HD
                ]


def encode_body(pos, gain, bias, *refs):
    blocks, held, out, tile = refs[:RING], refs[RING : RING + 2], refs[RING + 2], refs[RING + 3]
    assemble_rows(pos, blocks, tile)
    value = tile[...].astype(F32)
    center = jnp.mean(value, axis=-1, keepdims=True)
    value = value - center
    spread = jnp.mean(jnp.square(value), axis=-1, keepdims=True)
    normed = (value * lax.rsqrt(spread + 1e-05) * gain[...] + bias[...]).astype(BF)
    lane = lax.broadcasted_iota(jnp.int32, (TILE_ROWS, HALF), 1)
    scale = LOG2E / math.sqrt(VHD)
    for half in range(2):
        qkv = jnp.dot(normed, held[half][:DV, :], preferred_element_type=F32).astype(BF)
        query, key, value = qkv[:, :HALF], qkv[:, HALF : 2 * HALF], qkv[:, 2 * HALF : PART]
        context = jnp.zeros((TILE_ROWS, HALF), F32)
        for h in range(2):
            mine = (lane < VHD) == (h == 0)
            zero = jnp.zeros((), BF)
            scores = lax.dot_general(
                jnp.where(mine, query, zero), key, (((1,), (1,)), ((), ())), preferred_element_type=F32
            )
            highest = jnp.max(scores, axis=-1, keepdims=True)
            exponent = jnp.exp2((scores - highest) * scale)
            total = jnp.sum(exponent, axis=-1, keepdims=True)
            weight = (exponent / total).astype(BF)
            context = context + jnp.dot(weight, jnp.where(mine, value, zero), preferred_element_type=F32)
        out[:, half * HALF : (half + 1) * HALF] = context.astype(BF)


def project_body(pos, k_gain, w_out, w_kv, *refs):
    blocks, contexts = refs[:RING], refs[RING : 2 * RING]
    out, tile, held = refs[2 * RING :]
    assemble_rows(pos, blocks, tile)
    total = tile[...].astype(F32)
    for k in range(RING):
        part = (pos[1] - k + RING) % RING
        held[:HALF, :] = w_out[pl.ds(aligned(part * 2 + pos[2], HALF), HALF), :]
        held[HALF:, :] = w_out[pl.ds(aligned(part * 2 + 1 - pos[2], HALF), HALF), :]
        total = total + jnp.dot(contexts[k][...], held[...], preferred_element_type=F32)
    residual = total.astype(BF)
    key = jnp.dot(residual, w_kv[:, pl.ds(aligned(pos[1], HD), HD)], preferred_element_type=F32)
    value = jnp.dot(residual, w_kv[:, pl.ds(aligned(pos[1] + KVH, HD), HD)], preferred_element_type=F32)
    key = key * lax.rsqrt(jnp.mean(jnp.square(key), axis=-1, keepdims=True) + 1e-06) * k_gain[...]
    out[:, :HD] = key.astype(BF)
    out[:, HD:] = value.astype(BF)


BLOCK = 256
STACK = RING * GQ * 64


def softmax_rows(query, keys, values, seen):
    scores = lax.dot_general(query, keys, (((1,), (1,)), ((), ())), preferred_element_type=F32)
    scores = seen(scores)
    highest = jnp.max(scores, axis=-1, keepdims=True)
    exponent = jnp.exp2((scores - highest) * (LOG2E / math.sqrt(HD)))
    result = jnp.dot(exponent.astype(BF), values, preferred_element_type=F32)
    return (result[:, :HD] / result[:, HD:]).astype(BF)


def attend_rows(pos, packed, column, outs, held_q, held_o, held_k, held_v, seen_at):
    for k in range(RING):
        for h in range(GQ):
            lane = column + h * HD
            held_q[(k * GQ + h) * 64 : (k * GQ + h + 1) * 64, :HD] = packed[k][:, lane : lane + HD]

    def block(i, carry):
        at = pl.ds(pl.multiple_of(i * BLOCK, BLOCK), BLOCK)
        source = (pos[1] - i // (GQ * 64 // BLOCK) + RING) % RING
        row = lax.broadcasted_iota(jnp.int32, (BLOCK, 1), 0) % 64
        seen = seen_at(source * 128 + pos[2] * 64 + row)
        held_o[at, :] = softmax_rows(held_q[at, :], held_k[...], held_v[...], seen)
        return carry

    lax.fori_loop(0, STACK // BLOCK, block, 0, unroll=8)
    for k in range(RING):
        for h in range(GQ):
            outs[k][:, h * HD : (h + 1) * HD] = held_o[(k * GQ + h) * 64 : (k * GQ + h + 1) * 64, :]


def cross_body(pos, tpi, table, offsets, *refs):
    queries, sides, outs = refs[:RING], refs[RING : RING + 2], refs[RING + 2 : 2 * RING + 2]
    held_q, held_o, held_k, held_v = refs[2 * RING + 2 :]
    group = pos[3]
    images = [table[group * SLOTS + s] for s in range(SLOTS)]
    firsts = [first_of(tpi, image) for image in images]
    counts = [tpi[image] for image in images]
    held_v[:, HD:] = jnp.ones((STACK, HD), BF)
    lane = lax.broadcasted_iota(jnp.int32, (TILE_ROWS, HD), 1)
    for n in range(2 * RING):
        rows = slice(n * TILE_ROWS, (n + 1) * TILE_ROWS)
        side = slice(n % RING * TILE_ROWS, (n % RING + 1) * TILE_ROWS)
        held_k[rows, :HD] = sides[n // RING][side, :HD]
        held_v[rows, :HD] = sides[n // RING][side, HD:]
        entry = (pos[0] - n % RING + RING) % RING
        slot, u = entry // 2, entry % 2
        core = pos[2] if n < RING else 1 - pos[2]
        first = jnp.where(slot == 0, firsts[0], firsts[1])
        count = jnp.where(slot == 0, counts[0], counts[1])
        step = ((core + first) & 1) + 2 * u
        none = jnp.where(step < count, 0.0, LOW).astype(F32)
        late = jnp.where(slot == 0, 0.0, LOW).astype(F32)
        held_k[rows, HD:] = jnp.where(lane == 0, none, jnp.where(lane == 1, late, 0.0)).astype(BF)
    for k in range(RING):
        source = (pos[1] - k + RING) % RING
        row = lax.broadcasted_iota(jnp.int32, (64, HD), 0)
        column = lax.broadcasted_iota(jnp.int32, (64, HD), 1)
        position = offsets[group] + pos[0] * 512 + source * 128 + pos[2] * 64 + row
        before = jnp.where(position < SLOT_SPAN, 1.0, 0.0)
        extra = jnp.where(column == 0, 1.0, jnp.where(column == 1, before, 0.0)).astype(BF)
        for h in range(GQ):
            held_q[(k * GQ + h) * 64 : (k * GQ + h + 1) * 64, HD:] = extra
    attend_rows(pos, queries, Q_COLS, outs, held_q, held_o, held_k, held_v, lambda local: lambda scores: scores)


def self_body(pos, *refs):
    queries, sides, outs = refs[:RING], refs[RING : RING + 2], refs[RING + 2 : 2 * RING + 2]
    held_q, held_o, held_k, held_v = refs[2 * RING + 2 :]
    for n in range(2):
        for k in range(RING):
            at, row, lane = k * 512 + n * 256, DV + k % 2 * 256, k // 2 * 2 * HD
            held_k[at : at + 256, :] = sides[n][row : row + 256, lane : lane + HD]
            held_v[at : at + 256, :HD] = sides[n][row : row + 256, lane + HD : lane + 2 * HD]
    held_v[:, HD:] = jnp.ones((STACK, HD), BF)

    def seen_at(local):
        col = lax.broadcasted_iota(jnp.int32, (1, 512), 1)
        piece = col // 64
        core = jnp.where(piece < RING, pos[2], 1 - pos[2])
        key_at = (pos[1] - piece % RING + RING) % RING * 128 + core * 64 + col % 64

        def seen(scores):
            parts = [jnp.where(key_at <= local, scores[:, :512], LOW)]
            for k in range(1, RING):
                low = jnp.where(pos[0] >= k, 0.0, LOW).astype(F32)
                parts.append(scores[:, k * 512 : (k + 1) * 512] + low)
            return jnp.concatenate(parts, axis=1)

        return seen

    attend_rows(pos, queries, 0, outs, held_q, held_o, held_k, held_v, seen_at)


def place_body(pos, *refs):
    ins, out = refs[:RING], refs[RING]
    for k in range(RING):
        out[:, pl.ds(aligned((pos[1] + k) % RING, GQ * HD), GQ * HD)] = ins[k][...]


def per_device(
    tiles,
    w_qkv,
    w_out,
    w_kv,
    ln_gain,
    ln_bias,
    k_gain,
    cross_queries,
    self_queries,
    text_kv,
    tiles_per_image,
    request_table,
    span_offsets,
):
    dev = lax.axis_index("dev")
    pos = jnp.stack([dev // 8, (dev // 2) % 4, dev % 2, lax.axis_index("group")]).astype(jnp.int32)
    tpi = tiles_per_image.reshape(-1)
    table = request_table.reshape(-1)
    tokens = cross_queries.shape[0]
    ring = (1, 2, 3)

    held = chip_trade(tiles.reshape(TILE_ROWS, DV))
    mine, theirs = call(split_w_body, [jax.ShapeDtypeStruct((RING, 40, PART), BF)] * 2, (pos,), (w_qkv,))
    got = core_swap(theirs)
    even = pos[2] == 0
    pair = jnp.concatenate([jnp.where(even, mine, got), jnp.where(even, got, mine)], axis=1)
    parts = call(pack_parts_body, [shape(PART_ROWS, WIDE)] * RING, (pos,), (pair, text_kv))
    parts = [parts[0]] + [x_shift(parts[k], k) for k in ring]
    chosen = call(
        select_body, [shape(8 * 64, DV)], (pos, tpi, table), (held,), later=tuple(parts[1:])
    )[0]

    received = lax.all_to_all(chosen.reshape(8, 64, DV), "group", 0, 0, tiled=True).reshape(8 * 64, DV)
    joined = join(parts, later=(chosen,))
    back, ahead = z_shift(joined, 1), z_shift(joined, 3)
    far = 2 * PART_ROWS
    weights = (joined, back, ahead, z_shift(back[:far], 1), z_shift(ahead[far:], 3))

    heads = call(
        pack_heads_body,
        [shape(64, 2 * Q_COLS)] * RING,
        (pos,),
        (self_queries, cross_queries),
        later=(chosen,),
    )
    heads = [heads[0]] + [x_shift(heads[k], k) for k in ring]
    rows = z_trade(pick(pos, table, received, tuple(heads[1:])))
    blocks = [rows] + [x_shift(rows, k) for k in ring]
    half = call(weights_body, [shape(DV + 512, WIDE)], (pos,), weights, later=(rows,))[0]
    other = core_swap(half)
    context = call(
        encode_body,
        [shape(TILE_ROWS, 2 * HALF)],
        (pos,),
        (ln_gain.reshape(1, DV), ln_bias.reshape(1, DV), *blocks, half, other),
        [pltpu.VMEM((TILE_ROWS, DV), BF)],
        flops=1 << 30,
    )[0]
    contexts = [context] + [x_shift(context, k) for k in ring]
    own = call(
        self_body,
        [shape(64, Q_COLS)] * RING,
        (pos,),
        (*heads, half, other),
        [pltpu.VMEM((STACK, HD), BF)] * 3 + [pltpu.VMEM((STACK, 2 * HD), BF)],
        flops=1 << 32,
        later=(context,),
    )
    piece = call(
        project_body,
        [shape(TILE_ROWS, 2 * HD)],
        (pos,),
        (k_gain.reshape(1, HD), w_out, w_kv, *blocks, *contexts),
        [pltpu.VMEM((TILE_ROWS, DV), BF), pltpu.VMEM((2 * HALF, DV), BF)],
        flops=1 << 30,
        later=(own[0],),
    )[0]
    pieces = [piece] + [z_shift(piece, k) for k in ring]
    own = [own[0]] + [x_shift(own[k], RING - k) for k in ring]
    pieces = join(pieces, later=tuple(own[1:]))
    back = call(
        cross_body,
        [shape(64, Q_COLS)] * RING,
        (pos, tpi, table, span_offsets),
        (*heads, pieces, core_swap(pieces)),
        [pltpu.VMEM((STACK, 2 * HD), BF), pltpu.VMEM((STACK, HD), BF)] + [pltpu.VMEM((STACK, 2 * HD), BF)] * 2,
        flops=1 << 32,
    )
    back = [back[0]] + [x_shift(back[k], RING - k) for k in ring]
    self_out = call(place_body, [shape(tokens, RING * Q_COLS)], (pos,), tuple(own), later=(back[0],))[0]
    cross_out = call(place_body, [shape(tokens, RING * Q_COLS)], (pos,), tuple(back))[0]
    return (cross_out, self_out)


def solution(mesh):
    in_specs = (
        P(("group", "dev"), None, None),
        P("dev", None),
        P(),
        P(),
        P(),
        P(),
        P(),
        P(("group", "dev"), None),
        P(("group", "dev"), None),
        P(("group", "dev"), None),
        P(),
        P(),
        P(),
    )
    out_specs = (P(("group", "dev"), None), P(("group", "dev"), None))
    return jax.shard_map(
        per_device, mesh=mesh, in_specs=in_specs, out_specs=out_specs, check_vma=False
    )
```

```python
import math

import jax
import jax.numpy as jnp
from jax import lax
from jax.experimental import pallas as pl
from jax.experimental.pallas import tpu as pltpu
from jax.sharding import PartitionSpec as P

RING = 4
VHD = 80
HD = 128
KVH = 4
GQ = 8
SLOTS = 2
IMG_G = 16
TILE_ROWS = 256
DV = 1280
PART = 480
WIDE = 512
HALF = 160
SLOT_SPAN = 1024
LOG2E = math.log2(math.e)
LOW = -1e30
BF = jnp.bfloat16
F32 = jnp.float32
VM = pl.BlockSpec(memory_space=pltpu.VMEM)
SM = pl.BlockSpec(memory_space=pltpu.SMEM)


def shape(rows, cols):
    return jax.ShapeDtypeStruct((rows, cols), BF)


def call(body, outs, scalars, arrays, scratch=(), limit=40, flops=0, later=()):
    count, skip = len(scalars) + len(arrays), len(later)

    def without(*refs):
        body(*refs[:count], *refs[count + skip :])

    return pl.pallas_call(
        without,
        out_shape=outs,
        in_specs=[SM] * len(scalars) + [VM] * len(arrays) + [pl.BlockSpec(memory_space=pl.ANY)] * skip,
        out_specs=[VM] * len(outs),
        scratch_shapes=list(scratch),
        compiler_params=pltpu.CompilerParams(vmem_limit_bytes=limit << 20),
        cost_estimate=pl.CostEstimate(flops=flops, bytes_accessed=1 << 20, transcendentals=0),
    )(*scalars, *arrays, *later)


def x_shift(value, k):
    return lax.ppermute(value, "dev", [(i, (i // 8) * 8 + (i + 2 * k) % 8) for i in range(32)])


def z_shift(value, k):
    return lax.ppermute(value, "dev", [(i, (i + 8 * k) % 32) for i in range(32)])


def chip_trade(value):
    groups = [[chip * 2 + c for chip in range(RING * RING)] for c in range(2)]
    return lax.all_to_all(value, "dev", 0, 0, tiled=True, axis_index_groups=groups)


def z_trade(value):
    groups = [[z * 8 + i for z in range(RING)] for i in range(8)]
    return lax.all_to_all(value, "dev", 0, 0, tiled=True, axis_index_groups=groups)


def core_swap(value):
    return lax.ppermute(value, "dev", [(i, i ^ 1) for i in range(32)])


def aligned(value, unit):
    return pl.multiple_of(value * unit, unit)


def first_of(tpi, image):
    row, col = image // IMG_G, image % IMG_G
    total = jnp.int32(0)
    for j in range(IMG_G):
        total = total + jnp.where(j < col, tpi[row * IMG_G + j], 0)
    return total


def select_body(pos, tpi, table, held, out):
    for item in range(8 * SLOTS):
        first = first_of(tpi, table[item])
        for u in range(2):
            step = ((pos[2] + first) & 1) + 2 * u
            chip = jnp.minimum(first + step, 31) // 2
            row = (item * 2 + u) * 16
            out[row : row + 16, :] = held[pl.ds(aligned(chip, 16), 16), :]


def pick_body(pos, table, received, out, sems):
    copies = []
    for z in range(RING):
        owner = table[pos[3] * SLOTS + z // 2] // IMG_G
        source = received.at[pl.ds(aligned(owner * RING + z, 16), 16), :]
        copies.append(pltpu.make_async_copy(source, out.at[16 * z : 16 * z + 16, :], sems.at[z]))
    for copy in copies:
        copy.start()
    for copy in copies:
        copy.wait()


def pick(pos, table, received, later):
    def without(*refs):
        pick_body(*refs[:3], *refs[3 + len(later) :])

    return pl.pallas_call(
        without,
        out_shape=shape(RING * 16, DV),
        in_specs=[SM, SM] + [pl.BlockSpec(memory_space=pl.ANY)] * (1 + len(later)),
        out_specs=VM,
        scratch_shapes=[pltpu.SemaphoreType.DMA((RING,))],
    )(pos, table, received, *later)


def join_body(*refs):
    size = refs[0].shape[0]
    for k in range(RING):
        refs[RING][k * size : (k + 1) * size, :] = refs[k][...]


def join(values, later=()):
    rows, cols = values[0].shape
    return call(join_body, [shape(RING * rows, cols)], (), tuple(values), later=later)[0]


def split_w_body(pos, w, mine, theirs):
    first = pos[2] == 0
    for p in range(RING):
        for j in range(3):
            at = j * DV + p * 2 * HALF
            lo, hi = w[:, at : at + HALF], w[:, at + HALF : at + 2 * HALF]
            mine[p, :, j * HALF : (j + 1) * HALF] = jnp.where(first, lo, hi)
            theirs[p, :, j * HALF : (j + 1) * HALF] = jnp.where(first, hi, lo)


Q_COLS = GQ * HD
KV_AT = 2 * Q_COLS
TEXT_ROWS = 32
PART_ROWS = 80 + TEXT_ROWS


def pack_parts_body(pos, pair, text, *outs):
    for k in range(RING):
        head = (pos[1] + k) % RING
        outs[k][:80, :PART] = pair[head]
        outs[k][:80, PART:] = jnp.zeros((80, WIDE - PART), BF)
        for n in range(2):
            rows, at = slice(n * TEXT_ROWS, (n + 1) * TEXT_ROWS), n * 2 * HD
            outs[k][80:, at : at + HD] = text[rows, pl.ds(aligned(head, HD), HD)]
            outs[k][80:, at + HD : at + 2 * HD] = text[rows, pl.ds(aligned(head + KVH, HD), HD)]


def pack_heads_body(pos, own, asked, *outs):
    for k in range(RING):
        head = (pos[1] + k) % RING
        outs[k][:, :Q_COLS] = own[:, pl.ds(aligned(head, Q_COLS), Q_COLS)]
        outs[k][:, Q_COLS:] = asked[:, pl.ds(aligned(head, Q_COLS), Q_COLS)]


def assemble_rows(pos, blocks, tile):
    for k in range(RING):
        tile[pl.ds(aligned((pos[1] - k + RING) % RING, 64), 64), :] = blocks[k][...]


def weights_body(pos, mine, back, ahead, far_a, far_b, out):
    for zk, refs in ((0, (mine,)), (1, (back,)), (3, (ahead,)), (2, (far_a, far_b))):
        for xk in range(RING):
            row = ((pos[0] - zk + RING) % RING) * RING + (pos[1] - xk + RING) % RING
            ref = refs[xk * len(refs) // RING]
            at = PART_ROWS * (xk if len(refs) == 1 else xk % 2)
            out[pl.ds(aligned(row, 80), 80), :] = ref[at : at + 80, :]
            for n in range(2):
                to, lane = DV + zk % 2 * 256 + xk * 64 + n * TEXT_ROWS, zk // 2 * 2 * HD
                out[to : to + TEXT_ROWS, lane : lane + 2 * HD] = ref[
                    at + 80 : at + PART_ROWS, n * 2 * HD : (n + 1) * 2 * HD
                ]


def encode_body(pos, gain, bias, *refs):
    blocks, held, out, tile = refs[:RING], refs[RING : RING + 2], refs[RING + 2], refs[RING + 3]
    assemble_rows(pos, blocks, tile)
    value = tile[...].astype(F32)
    center = jnp.mean(value, axis=-1, keepdims=True)
    value = value - center
    spread = jnp.mean(jnp.square(value), axis=-1, keepdims=True)
    normed = (value * lax.rsqrt(spread + 1e-05) * gain[...] + bias[...]).astype(BF)
    lane = lax.broadcasted_iota(jnp.int32, (TILE_ROWS, HALF), 1)
    scale = LOG2E / math.sqrt(VHD)
    for half in range(2):
        qkv = jnp.dot(normed, held[half][:DV, :], preferred_element_type=F32).astype(BF)
        query, key, value = qkv[:, :HALF], qkv[:, HALF : 2 * HALF], qkv[:, 2 * HALF : PART]
        context = jnp.zeros((TILE_ROWS, HALF), F32)
        for h in range(2):
            mine = (lane < VHD) == (h == 0)
            zero = jnp.zeros((), BF)
            scores = lax.dot_general(
                jnp.where(mine, query, zero), key, (((1,), (1,)), ((), ())), preferred_element_type=F32
            )
            highest = jnp.max(scores, axis=-1, keepdims=True)
            exponent = jnp.exp2((scores - highest) * scale)
            total = jnp.sum(exponent, axis=-1, keepdims=True)
            weight = (exponent / total).astype(BF)
            context = context + jnp.dot(weight, jnp.where(mine, value, zero), preferred_element_type=F32)
        out[:, half * HALF : (half + 1) * HALF] = context.astype(BF)


def project_body(pos, k_gain, w_out, w_kv, *refs):
    blocks, contexts = refs[:RING], refs[RING : 2 * RING]
    out, tile, held = refs[2 * RING :]
    assemble_rows(pos, blocks, tile)
    total = tile[...].astype(F32)
    for k in range(RING):
        part = (pos[1] - k + RING) % RING
        held[:HALF, :] = w_out[pl.ds(aligned(part * 2 + pos[2], HALF), HALF), :]
        held[HALF:, :] = w_out[pl.ds(aligned(part * 2 + 1 - pos[2], HALF), HALF), :]
        total = total + jnp.dot(contexts[k][...], held[...], preferred_element_type=F32)
    residual = total.astype(BF)
    key = jnp.dot(residual, w_kv[:, pl.ds(aligned(pos[1], HD), HD)], preferred_element_type=F32)
    value = jnp.dot(residual, w_kv[:, pl.ds(aligned(pos[1] + KVH, HD), HD)], preferred_element_type=F32)
    key = key * lax.rsqrt(jnp.mean(jnp.square(key), axis=-1, keepdims=True) + 1e-06) * k_gain[...]
    out[:, :HD] = key.astype(BF)
    out[:, HD:] = value.astype(BF)


BLOCK = 256
STACK = RING * GQ * 64


def softmax_rows(query, keys, values, seen):
    scores = lax.dot_general(query, keys, (((1,), (1,)), ((), ())), preferred_element_type=F32)
    scores = seen(scores)
    highest = jnp.max(scores, axis=-1, keepdims=True)
    exponent = jnp.exp2((scores - highest) * (LOG2E / math.sqrt(HD)))
    result = jnp.dot(exponent.astype(BF), values, preferred_element_type=F32)
    return (result[:, :HD] / result[:, HD:]).astype(BF)


def attend_rows(pos, packed, column, outs, held_q, held_o, held_k, held_v, seen_at):
    for k in range(RING):
        for h in range(GQ):
            lane = column + h * HD
            held_q[(k * GQ + h) * 64 : (k * GQ + h + 1) * 64, :HD] = packed[k][:, lane : lane + HD]

    def block(i, carry):
        at = pl.ds(pl.multiple_of(i * BLOCK, BLOCK), BLOCK)
        source = (pos[1] - i // (GQ * 64 // BLOCK) + RING) % RING
        row = lax.broadcasted_iota(jnp.int32, (BLOCK, 1), 0) % 64
        seen = seen_at(source * 128 + pos[2] * 64 + row)
        held_o[at, :] = softmax_rows(held_q[at, :], held_k[...], held_v[...], seen)
        return carry

    lax.fori_loop(0, STACK // BLOCK, block, 0, unroll=8)
    for k in range(RING):
        for h in range(GQ):
            outs[k][:, h * HD : (h + 1) * HD] = held_o[(k * GQ + h) * 64 : (k * GQ + h + 1) * 64, :]


def cross_body(pos, tpi, table, offsets, *refs):
    queries, sides, outs = refs[:RING], refs[RING : RING + 2], refs[RING + 2 : 2 * RING + 2]
    held_q, held_o, held_k, held_v = refs[2 * RING + 2 :]
    group = pos[3]
    images = [table[group * SLOTS + s] for s in range(SLOTS)]
    firsts = [first_of(tpi, image) for image in images]
    counts = [tpi[image] for image in images]
    held_v[:, HD:] = jnp.ones((STACK, HD), BF)
    lane = lax.broadcasted_iota(jnp.int32, (TILE_ROWS, HD), 1)
    for n in range(2 * RING):
        rows = slice(n * TILE_ROWS, (n + 1) * TILE_ROWS)
        side = slice(n % RING * TILE_ROWS, (n % RING + 1) * TILE_ROWS)
        held_k[rows, :HD] = sides[n // RING][side, :HD]
        held_v[rows, :HD] = sides[n // RING][side, HD:]
        entry = (pos[0] - n % RING + RING) % RING
        slot, u = entry // 2, entry % 2
        core = pos[2] if n < RING else 1 - pos[2]
        first = jnp.where(slot == 0, firsts[0], firsts[1])
        count = jnp.where(slot == 0, counts[0], counts[1])
        step = ((core + first) & 1) + 2 * u
        none = jnp.where(step < count, 0.0, LOW).astype(F32)
        late = jnp.where(slot == 0, 0.0, LOW).astype(F32)
        held_k[rows, HD:] = jnp.where(lane == 0, none, jnp.where(lane == 1, late, 0.0)).astype(BF)
    for k in range(RING):
        source = (pos[1] - k + RING) % RING
        row = lax.broadcasted_iota(jnp.int32, (64, HD), 0)
        column = lax.broadcasted_iota(jnp.int32, (64, HD), 1)
        position = offsets[group] + pos[0] * 512 + source * 128 + pos[2] * 64 + row
        before = jnp.where(position < SLOT_SPAN, 1.0, 0.0)
        extra = jnp.where(column == 0, 1.0, jnp.where(column == 1, before, 0.0)).astype(BF)
        for h in range(GQ):
            held_q[(k * GQ + h) * 64 : (k * GQ + h + 1) * 64, HD:] = extra
    attend_rows(pos, queries, Q_COLS, outs, held_q, held_o, held_k, held_v, lambda local: lambda scores: scores)


def self_body(pos, *refs):
    queries, sides, outs = refs[:RING], refs[RING : RING + 2], refs[RING + 2 : 2 * RING + 2]
    held_q, held_o, held_k, held_v = refs[2 * RING + 2 :]
    for n in range(2):
        for k in range(RING):
            at, row, lane = k * 512 + n * 256, DV + k % 2 * 256, k // 2 * 2 * HD
            held_k[at : at + 256, :] = sides[n][row : row + 256, lane : lane + HD]
            held_v[at : at + 256, :HD] = sides[n][row : row + 256, lane + HD : lane + 2 * HD]
    held_v[:, HD:] = jnp.ones((STACK, HD), BF)

    def seen_at(local):
        col = lax.broadcasted_iota(jnp.int32, (1, 512), 1)
        piece = col // 64
        core = jnp.where(piece < RING, pos[2], 1 - pos[2])
        key_at = (pos[1] - piece % RING + RING) % RING * 128 + core * 64 + col % 64

        def seen(scores):
            parts = [jnp.where(key_at <= local, scores[:, :512], LOW)]
            for k in range(1, RING):
                low = jnp.where(pos[0] >= k, 0.0, LOW).astype(F32)
                parts.append(scores[:, k * 512 : (k + 1) * 512] + low)
            return jnp.concatenate(parts, axis=1)

        return seen

    attend_rows(pos, queries, 0, outs, held_q, held_o, held_k, held_v, seen_at)


def place_body(pos, *refs):
    ins, out = refs[:RING], refs[RING]
    for k in range(RING):
        out[:, pl.ds(aligned((pos[1] + k) % RING, GQ * HD), GQ * HD)] = ins[k][...]


def per_device(
    tiles,
    w_qkv,
    w_out,
    w_kv,
    ln_gain,
    ln_bias,
    k_gain,
    cross_queries,
    self_queries,
    text_kv,
    tiles_per_image,
    request_table,
    span_offsets,
):
    dev = lax.axis_index("dev")
    pos = jnp.stack([dev // 8, (dev // 2) % 4, dev % 2, lax.axis_index("group")]).astype(jnp.int32)
    tpi = tiles_per_image.reshape(-1)
    table = request_table.reshape(-1)
    tokens = cross_queries.shape[0]
    ring = (1, 2, 3)

    held = chip_trade(tiles.reshape(TILE_ROWS, DV))
    mine, theirs = call(split_w_body, [jax.ShapeDtypeStruct((RING, 40, PART), BF)] * 2, (pos,), (w_qkv,))
    got = core_swap(theirs)
    even = pos[2] == 0
    pair = jnp.concatenate([jnp.where(even, mine, got), jnp.where(even, got, mine)], axis=1)
    parts = call(pack_parts_body, [shape(PART_ROWS, WIDE)] * RING, (pos,), (pair, text_kv))
    parts = [parts[0]] + [x_shift(parts[k], k) for k in ring]
    chosen = call(
        select_body, [shape(8 * 64, DV)], (pos, tpi, table), (held,), later=tuple(parts[1:])
    )[0]

    received = lax.all_to_all(chosen.reshape(8, 64, DV), "group", 0, 0, tiled=True).reshape(8 * 64, DV)
    joined = join(parts, later=(chosen,))
    back, ahead = z_shift(joined, 1), z_shift(joined, 3)
    far = 2 * PART_ROWS
    weights = (joined, back, ahead, z_shift(back[:far], 1), z_shift(ahead[far:], 3))

    heads = call(
        pack_heads_body,
        [shape(64, 2 * Q_COLS)] * RING,
        (pos,),
        (self_queries, cross_queries),
        later=(chosen,),
    )
    heads = [heads[0]] + [x_shift(heads[k], k) for k in ring]
    rows = z_trade(pick(pos, table, received, tuple(heads[1:])))
    blocks = [rows] + [x_shift(rows, k) for k in ring]
    half = call(weights_body, [shape(DV + 512, WIDE)], (pos,), weights, later=(rows,))[0]
    other = core_swap(half)
    context = call(
        encode_body,
        [shape(TILE_ROWS, 2 * HALF)],
        (pos,),
        (ln_gain.reshape(1, DV), ln_bias.reshape(1, DV), *blocks, half, other),
        [pltpu.VMEM((TILE_ROWS, DV), BF)],
        flops=1 << 30,
    )[0]
    contexts = [context] + [x_shift(context, k) for k in ring]
    own = call(
        self_body,
        [shape(64, Q_COLS)] * RING,
        (pos,),
        (*heads, half, other),
        [pltpu.VMEM((STACK, HD), BF)] * 3 + [pltpu.VMEM((STACK, 2 * HD), BF)],
        flops=1 << 32,
        later=(context,),
    )
    piece = call(
        project_body,
        [shape(TILE_ROWS, 2 * HD)],
        (pos,),
        (k_gain.reshape(1, HD), w_out, w_kv, *blocks, *contexts),
        [pltpu.VMEM((TILE_ROWS, DV), BF), pltpu.VMEM((2 * HALF, DV), BF)],
        flops=1 << 30,
        later=(own[0],),
    )[0]
    pieces = [piece] + [z_shift(piece, k) for k in ring]
    own = [own[0]] + [x_shift(own[k], RING - k) for k in ring]
    pieces = join(pieces)
    back = call(
        cross_body,
        [shape(64, Q_COLS)] * RING,
        (pos, tpi, table, span_offsets),
        (*heads, pieces, core_swap(pieces)),
        [pltpu.VMEM((STACK, 2 * HD), BF), pltpu.VMEM((STACK, HD), BF)] + [pltpu.VMEM((STACK, 2 * HD), BF)] * 2,
        flops=1 << 32,
    )
    back = [back[0]] + [x_shift(back[k], RING - k) for k in ring]
    self_out = call(place_body, [shape(tokens, RING * Q_COLS)], (pos,), tuple(own), later=(back[0],))[0]
    cross_out = call(place_body, [shape(tokens, RING * Q_COLS)], (pos,), tuple(back))[0]
    return (cross_out, self_out)


def solution(mesh):
    in_specs = (
        P(("group", "dev"), None, None),
        P("dev", None),
        P(),
        P(),
        P(),
        P(),
        P(),
        P(("group", "dev"), None),
        P(("group", "dev"), None),
        P(("group", "dev"), None),
        P(),
        P(),
        P(),
    )
    out_specs = (P(("group", "dev"), None), P(("group", "dev"), None))
    return jax.shard_map(
        per_device, mesh=mesh, in_specs=in_specs, out_specs=out_specs, check_vma=False
    )
```
